1024 devices in a mesh: grp: 4 (over y), dom: 64 (over z, core), lev: 4 (over x).
Axes of the slice: x: 4, y: 4, z: 32, core: 2. Of those that a mesh axis runs over, the one named last changes fastest.
Arguments:
- atm_surface: bfloat16 [12, 1048576], P('lev', ('grp', 'dom')), may hold values from -12 to 12
- atm_levels: bfloat16 [80, 1048576], P('lev', ('grp', 'dom')), may hold values from -12 to 12
- margin_weights: bfloat16 [256, 8, 64, 2048], P(('grp', 'dom')), may hold values from 0 to 0.0625
- src_block: int32 [256, 8, 32], P(('grp', 'dom')), may hold values from 0 to 63
- dst_block: int32 [256, 8, 32], P(('grp', 'dom')), may hold values from -1 to 31, as said below
- ice_cover: float32 [524288], P(('grp', 'dom')), may hold values from 0 to 1
- ice_flux: bfloat16 [12, 524288], P('lev', ('grp', 'dom')), may hold values from -6 to 6
- ocean_state: bfloat16 [12, 524288], P('lev', ('grp', 'dom')), may hold values from -6 to 6
- drag: float32 [524288], P(('grp', 'dom')), may hold values from 0.5 to 2
- level_weights: float32 [80], P('lev'), may hold values from 0.025 to 0.225
- neighbours: int32 [524288, 6], P(('grp', 'dom')), may hold values from 0 to 2303, as said below
Outputs:
- ocean_surface: float32 [12, 524288], P('lev', ('grp', 'dom'))
- ocean_levels: float32 [80, 524288], P('lev', ('grp', 'dom'))
- atm_flux: float32 [12, 1048576], P('lev', ('grp', 'dom'))
The draws below stay inside these ranges and needn't reach their ends.
Inputs may be any that keep to these rules, and one draw needn't show every extreme that they name: `dst_block`: -1 marks an unused slot. `neighbours`: entry e names the partition's cell e - 128, counted from the partition's first cell, so values below 128 reach into the previous partition of the region group and values of 2176 or more into the next.
All inputs are finite; a program needn't handle non-finite values.
Results may differ from the reference program's by a relative error of at most 0.0034.
Values may be sent and summed in bfloat16 or wider, within the bound.
A program may use at most 64 MiB of HBM per device.

```python
import math
import jax
import jax.numpy as jnp
from jax import lax

SURF = 12
LEVELS = 80
BLK = 64
NEAR = 8
CAP = 32
NB = 6
HW = 128
SB = 64
TB = 32
NPART = 256
CYCLE = 131072
ATM_COLS = 1048576
OCN_CELLS = 524288


def draw_src_block(key, part):
    key = jax.random.fold_in(key, 11)
    picks = jax.random.randint(key, (NPART, NEAR, CAP), 0, SB, dtype=jnp.int32)
    picks = picks.at[0, 0, 0].set(SB - 1)
    return picks.at[0, 1, 0].set(0)


def draw_dst_block(key, part):
    key = jax.random.fold_in(key, 23)
    key_load, key_roll, key_pick = jax.random.split(key, 3)
    load_target = jax.random.randint(key_load, (NPART,), 1, 5, dtype=jnp.int32)
    target_ids = (jnp.arange(NPART, dtype=jnp.int32)[:, None] + jnp.arange(NEAR, dtype=jnp.int32)[None, :]) % NPART
    load = load_target[target_ids][:, :, None]
    rolled = jax.random.randint(key_roll, (NPART, NEAR, CAP), 0, 4, dtype=jnp.int32)
    picks = jax.random.randint(key_pick, (NPART, NEAR, CAP), 0, TB, dtype=jnp.int32)
    picks = jnp.where(rolled < load, picks, -1)
    picks = picks.at[0, 0, 0].set(TB - 1)
    return picks.at[0, 0, 1].set(-1)


def draw_neighbours(key, part):
    key = jax.random.fold_in(key, 37)
    key_reach, key_sign = jax.random.split(key)
    reach = jax.random.randint(key_reach, (OCN_CELLS, NB), 1, HW + 1, dtype=jnp.int32)
    sign = 2 * jax.random.randint(key_sign, (OCN_CELLS, NB), 0, 2, dtype=jnp.int32) - 1
    local = (jnp.arange(OCN_CELLS, dtype=jnp.int32) % (TB * BLK))[:, None]
    named = local + sign * reach + HW
    column_zero = jnp.arange(NB, dtype=jnp.int32)[None, :] == 0
    named = jnp.where(column_zero & (local == 0), 0, named)
    named = jnp.where(column_zero & (local == TB * BLK - 1), TB * BLK + 2 * HW - 1, named)
    return named


def draw_level_weights(key, part):
    key = jax.random.fold_in(key, 41)
    rising = 1.0 + 2.0 * jnp.arange(LEVELS, dtype=jnp.float32) / (LEVELS - 1)
    return 0.05 * rising * jax.random.uniform(key, (LEVELS,), jnp.float32, 0.5, 1.5)


def steps_of(key, dims, cuts, low, high):
    level, own = 1.0, jax.random.fold_in(key, 6)
    for axis_at, blocks in cuts:
        draws = jnp.exp(jax.random.uniform(jax.random.fold_in(own, axis_at), (blocks,), jnp.float32, low / len(cuts), high / len(cuts)))
        level = level * jnp.repeat(draws, dims[axis_at] // blocks).reshape([-1 if axis == axis_at else 1 for axis in range(len(dims))])
    return level


def noise(rng, shape, deviation, limit, cuts=(), kind=jnp.bfloat16):
    drawn = deviation * jax.random.normal(rng, shape, jnp.float32)
    if cuts:
        drawn = drawn * steps_of(rng, shape, cuts, -0.22, 0.18)
    return jnp.clip(drawn, -limit, limit).astype(kind)


def setup_inputs(seed: int = 0) -> dict:
    streams_of = jax.random.split(jax.random.key(seed), 12)
    return {
        "atm_surface": noise(streams_of[0], (SURF, ATM_COLS), 2.0, 12.0, ((0, 4), (1, 256))),
        "atm_levels": noise(streams_of[1], (LEVELS, ATM_COLS), 2.0, 12.0, ((0, 4), (1, 256))),
        "margin_weights": jnp.clip(0.0625 * jax.random.uniform(streams_of[2], (NPART, NEAR, BLK, CAP * BLK), jnp.float32) ** steps_of(streams_of[2], (NPART, NEAR, BLK, CAP * BLK), ((0, 256),), -0.2, 0.2), 0.0, 0.0625).astype(jnp.bfloat16),
        "src_block": draw_src_block(jax.random.fold_in(streams_of[11], 71), 0),
        "dst_block": draw_dst_block(jax.random.fold_in(streams_of[11], 71), 0),
        "ice_cover": jnp.clip(1.0 * jax.random.uniform(streams_of[5], (OCN_CELLS,), jnp.float32) ** steps_of(streams_of[5], (OCN_CELLS,), ((0, 256),), -0.2, 0.2), 0.0, 1.0),
        "ice_flux": noise(streams_of[6], (SURF, OCN_CELLS), 1.0, 6.0, ((0, 4), (1, 256))),
        "ocean_state": noise(streams_of[7], (SURF, OCN_CELLS), 1.0, 6.0, ((0, 4), (1, 256))),
        "drag": jnp.clip(jnp.exp(math.log(2.0) - 1.3862944 * jax.random.uniform(streams_of[8], (OCN_CELLS,), jnp.float32) ** steps_of(streams_of[8], (OCN_CELLS,), ((0, 256),), -0.2, 0.2)), 0.5, 2.0),
        "level_weights": draw_level_weights(jax.random.fold_in(streams_of[11], 71), 0),
        "neighbours": draw_neighbours(jax.random.fold_in(streams_of[11], 71), 0),
    }


KAPPA = 0.5


def reference(atm_surface, atm_levels, margin_weights, src_block, dst_block, ice_cover, ice_flux, ocean_state, drag, level_weights, neighbours):
    chans = SURF + LEVELS
    fields = jnp.concatenate([atm_surface, atm_levels], axis=0)
    blocks = fields.reshape(chans, NPART, SB, BLK)
    offsets = jnp.arange(NEAR, dtype=jnp.int32)

    def target_rows(part_id):
        return ((part_id + offsets) % NPART)[:, None] * jnp.ones((1, CAP), jnp.int32)

    def forward(part_id, total):
        local = lax.dynamic_index_in_dim(blocks, part_id, 1, keepdims=False)
        picked = local[:, src_block[part_id], :]
        weight_mat = margin_weights[part_id].reshape(NEAR, BLK, CAP, BLK).astype(jnp.float32)
        pieces = jnp.einsum("kdci,dicj->kdcj", picked.astype(jnp.float32), weight_mat, precision=lax.Precision.HIGHEST).astype(jnp.bfloat16)
        targets = dst_block[part_id]
        valid = targets >= 0
        term = jnp.where(valid[None, :, :, None], pieces.astype(jnp.float32), jnp.zeros((), jnp.float32))
        return total.at[:, target_rows(part_id), jnp.maximum(targets, 0), :].add(term)

    total = lax.fori_loop(0, NPART, forward, jnp.zeros((chans, NPART, TB, BLK), jnp.float32))
    remapped = total.reshape(chans, NPART * TB * BLK)
    surface = (1.0 - ice_cover[None, :]) * remapped[:SURF] + ice_cover[None, :] * ice_flux.astype(jnp.float32)
    merged = jnp.concatenate([surface, remapped[SURF:]], axis=0).astype(jnp.bfloat16)
    cells = jnp.arange(NPART * TB * BLK, dtype=jnp.int32)
    base = cells - cells % CYCLE
    place = cells % CYCLE - cells % (TB * BLK)
    named = base[:, None] + (place[:, None] + neighbours - HW) % CYCLE
    beside_all = jnp.zeros((chans, NPART * TB * BLK), jnp.float32)
    for slot in range(NB):
        beside_all = beside_all + merged[:, named[:, slot]].astype(jnp.float32)
    beside_all = beside_all / NB
    centre = merged.astype(jnp.float32)
    forcing = centre + KAPPA * (beside_all - centre)
    column = jnp.sum(level_weights[:, None] * forcing[SURF:], axis=0)
    flux = (drag[None, :] * (ocean_state.astype(jnp.float32) - forcing[:SURF] + column[None, :])).astype(jnp.bfloat16)
    flux_blocks = flux.reshape(SURF, NPART, TB, BLK)

    def backward(part_id):
        targets = dst_block[part_id]
        valid = targets >= 0
        gathered = flux_blocks[:, target_rows(part_id), jnp.maximum(targets, 0), :].astype(jnp.float32)
        gathered = jnp.where(valid[None, :, :, None], gathered, jnp.zeros((), jnp.float32))
        weight_mat = margin_weights[part_id].reshape(NEAR, BLK, CAP, BLK).astype(jnp.float32)
        spread = jnp.einsum("sdcj,dicj->sdci", gathered, weight_mat, precision=lax.Precision.HIGHEST)
        return jnp.zeros((SURF, SB, BLK), jnp.float32).at[:, src_block[part_id], :].add(spread)

    back = lax.map(backward, jnp.arange(NPART, dtype=jnp.int32))
    atm_flux = jnp.transpose(back, (1, 0, 2, 3)).reshape(SURF, NPART * SB * BLK)
    return forcing[:SURF], forcing[SURF:], atm_flux
```

```python
import functools

import jax
import jax.numpy as jnp
from jax import lax
from jax.experimental import pallas as pl
from jax.experimental.pallas import tpu as pltpu
from jax.sharding import PartitionSpec as P

HW = 128
KAPPA = 0.5
ROWS = 24
MESH = pl.DeviceIdType.MESH
F32 = jnp.float32
BF16 = jnp.bfloat16


def dot(a, b):
    return jnp.dot(a, b, preferred_element_type=F32)


def forward_kernel(src, dst, surf_ref, lev_ref, w_ref, out_ref, joint, blocks, even, odd):
    o = pl.program_id(0)
    levels, surf = lev_ref.shape[0], surf_ref.shape[0]
    width = w_ref.shape[2]
    slots = w_ref.shape[3] // width
    count = even.shape[0] - 1

    @pl.when(o == 0)
    def _():
        joint[...] = jnp.zeros_like(joint)
        joint[0:levels, :] = lev_ref[...].astype(F32)
        joint[levels : levels + surf, :] = surf_ref[...].astype(F32)
        for pair in range(blocks.shape[0] // 2):
            both = joint[:, pair * 128 : pair * 128 + 128].astype(BF16)
            blocks[2 * pair] = both[:, :64]
            blocks[2 * pair + 1] = both[:, 64:]

    even[...] = jnp.zeros_like(even)
    odd[...] = jnp.zeros_like(odd)
    for pair in range(slots // 2):
        a, b = 2 * pair, 2 * pair + 1
        lhs = jnp.concatenate([blocks[src[0, o, a]], blocks[src[0, o, b]]], axis=0)
        got = dot(lhs, w_ref[0, 0, :, pair * 128 : pair * 128 + 128]).astype(BF16).astype(F32)
        to_a, to_b = dst[0, o, a], dst[0, o, b]
        to_a = jnp.where(to_a < 0, count, to_a)
        to_b = jnp.where(to_b < 0, count, to_b)
        even[to_a] = even[to_a] + got[:ROWS]
        odd[to_b] = odd[to_b] + got[32 : 32 + ROWS]
    low = lax.broadcasted_iota(jnp.int32, (ROWS, 128), 1) < 64

    def joined(t):
        left = even[2 * t] + pltpu.roll(odd[2 * t], 64, 1)
        right = pltpu.roll(even[2 * t + 1], 64, 1) + odd[2 * t + 1]
        return jnp.where(low, left, right)

    for t in range(0, count // 2, 2):
        both = jnp.concatenate([joined(t), joined(t + 1)], axis=0)
        out_ref[0, t * ROWS : (t + 2) * ROWS, :] = both.astype(BF16)


def middle_kernel(
    grp_n, dom_n, lev_n,
    agg, ice_cover, ice_flux, ocean_state, drag, level_weights, named,
    surf_out, lev_out, flux_out,
    sib, comb, recv, own, halo, counts, around, ice8, state8, lw_rows, surf8, flat, flux_send, flux_recv, col_send, col_recv,
    sib_s, sib_r, far_s, far_r, halo_s, halo_r, col_s, col_r, flux_s, flux_r,
):
    grp, dom, lev = lax.axis_index("grp"), lax.axis_index("dom"), lax.axis_index("lev")
    parts = grp_n * dom_n
    p = grp * dom_n + dom
    core = lax.rem(dom, 2)
    levels, surf = lev_out.shape[0], surf_out.shape[0]
    cells = lev_out.shape[1]
    tiles = cells // 128
    near = agg.shape[0]

    def part(by):
        q = lax.rem(p + by + parts, parts)
        return (q // dom_n, lax.rem(q, dom_n), lev)

    def ring(by):
        return (grp, lax.rem(dom + by + dom_n, dom_n), lev)

    def column_peer(by):
        return (grp, dom, lax.rem(lev + by, lev_n))

    sibling = (grp, dom + 1 - 2 * core, lev)

    barrier = pltpu.get_barrier_semaphore()
    greeted = 0
    for by in range(1, near + 1):
        for sign in (1, -1):
            pl.semaphore_signal(barrier, inc=1, device_id=part(sign * by), device_id_type=MESH)
            greeted += 1
    for by in (1, -1):
        pl.semaphore_signal(barrier, inc=1, device_id=ring(by), device_id_type=MESH)
        greeted += 1
    for by in range(1, lev_n):
        pl.semaphore_signal(barrier, inc=1, device_id=column_peer(by), device_id_type=MESH)
        greeted += 1
    pl.semaphore_wait(barrier, greeted)

    def copy(src, dst, send, got, device):
        return pltpu.make_async_remote_copy(
            src_ref=src, dst_ref=dst, send_sem=send, recv_sem=got, device_id=device, device_id_type=MESH
        )

    half = near // 2
    sib_copies = [copy(agg.at[2 * m + 1], sib.at[m], sib_s.at[m], sib_r.at[m], sibling) for m in range(half)]
    far_copies = [copy(comb.at[d - 1], recv.at[d - 1], far_s.at[d - 1], far_r.at[d - 1], part(2 * d)) for d in range(1, half)]
    last_copy = copy(sib.at[half - 1], recv.at[half - 1], far_s.at[half - 1], far_r.at[half - 1], part(2 * half))
    for m in reversed(range(half)):
        sib_copies[m].start()

    sib_copies[half - 1].wait_recv()

    @pl.when(core == 0)
    def _():
        last_copy.start()

    for d in reversed(range(1, half)):
        sib_copies[d - 1].wait_recv()
        comb[d - 1] = (agg[2 * d].astype(F32) + sib[d - 1 + core].astype(F32)).astype(BF16)
        far_copies[d - 1].start()

    def count_rows(i, carry):
        row = lax.broadcasted_iota(jnp.int32, (16, cells), 0) + i * 16
        total = jnp.zeros((16, cells), F32)
        for e in range(named.shape[0]):
            total = total + jnp.where(named[e : e + 1, :] == row, 1.0, 0.0)
        counts[pl.ds(pl.multiple_of(i * 16, 16), 16), :] = total.astype(BF16)
        return carry

    lax.fori_loop(0, counts.shape[0] // 16, count_rows, 0)

    first = levels - 16
    ice8[...] = jnp.zeros_like(ice8)
    state8[...] = jnp.zeros_like(state8)
    ice8[first : first + surf, :] = ice_flux[...].astype(F32)
    state8[first : first + surf, :] = ocean_state[...].astype(F32)
    lw_rows[...] = jnp.zeros_like(lw_rows)
    for k in range(levels):
        lw_rows[k : k + 1, :] = jnp.full((1, 128), level_weights[k], F32)

    for d in range(1, half):
        far_copies[d - 1].wait_recv()

    @pl.when(core == 0)
    def _():
        last_copy.wait_recv()

    @pl.when(core == 1)
    def _():
        recv[half - 1] = sib[0]

    is_surf = lax.broadcasted_iota(jnp.int32, (8, 128), 0) >= first
    for t in range(0, tiles, 2):
        rows = slice(t * ROWS, (t + 2) * ROWS)
        total = agg[0, rows, :].astype(F32)
        for d in range(half):
            total = total + recv[d, rows, :].astype(F32)
        for u in range(2):
            lanes = slice((t + u) * 128, (t + u + 1) * 128)
            one = total[u * ROWS : (u + 1) * ROWS]
            share = ice_cover[:, lanes]
            tail = jnp.where(is_surf, (1.0 - share) * one[16:] + share * ice8[:, lanes], one[16:])
            own[:, lanes] = jnp.concatenate([one[:16], tail, jnp.zeros((8, 128), F32)], axis=0).astype(BF16)

    to_prev = copy(own.at[:, 0:HW], halo.at[:, 0:HW], halo_s.at[0], halo_r.at[0], ring(-1))
    to_next = copy(own.at[:, cells - HW : cells], halo.at[:, HW : 2 * HW], halo_s.at[1], halo_r.at[1], ring(1))
    to_prev.start()
    to_next.start()
    for c in range(cells // 256):
        lanes = slice(c * 256, c * 256 + 256)
        around[:, lanes] = dot(own[...], counts[0:cells, lanes])
    to_prev.wait_recv()
    to_next.wait_recv()
    for c in range(cells // 256):
        lanes = slice(c * 256, c * 256 + 256)
        total = around[:, lanes] + dot(halo[...], counts[cells : cells + 2 * HW, lanes])
        forcing = (1.0 - KAPPA) * own[:, lanes].astype(F32) + (KAPPA / named.shape[0]) * total
        forcing = forcing[:ROWS]
        lev_out[:, lanes] = forcing[:levels]
        surf_out[:, lanes] = forcing[levels : levels + surf]
        surf8[:, lanes] = forcing[16:]
        weight = jnp.concatenate([lw_rows[...], lw_rows[...]], axis=1)
        col_send[:, lanes] = jnp.sum(weight * forcing, axis=0, keepdims=True)

    col_copies = [copy(col_send, col_recv.at[by - 1], col_s.at[by - 1], col_r.at[by - 1], column_peer(by)) for by in range(1, lev_n)]
    for one in col_copies:
        one.start()
    for one in col_copies:
        one.wait_recv()
    column = col_send[...]
    for by in range(1, lev_n):
        column = column + col_recv[by - 1]
    flux = drag[...] * (state8[...] - surf8[...] + column)
    for t in range(tiles):
        flat[t * surf : (t + 1) * surf, :] = flux[first : first + surf, t * 128 : t * 128 + 128]
    flux_send[...] = flat[...].astype(BF16)
    flux_copies = [copy(flux_send, flux_recv.at[o - 1], flux_s.at[o - 1], flux_r.at[o - 1], part(-o)) for o in range(1, near)]
    for one in reversed(flux_copies):
        one.start()
    flux_out[0] = flux_send[...]
    for o in range(1, near):
        flux_copies[o - 1].wait_recv()
        flux_out[o] = flux_recv[o - 1]

    for one in sib_copies + far_copies + [to_prev, to_next] + col_copies + flux_copies:
        one.wait_send()

    @pl.when(core == 0)
    def _():
        last_copy.wait_send()


def back_kernel(src, dst, flux_ref, w_ref, out_ref, flat, even, odd, total):
    o = pl.program_id(0)
    surf = out_ref.shape[0]
    width = w_ref.shape[2]
    slots = w_ref.shape[3] // width
    count = even.shape[0] - 1

    @pl.when(o == 0)
    def _():
        total[...] = jnp.zeros_like(total)
        even[...] = jnp.zeros_like(even)
        odd[...] = jnp.zeros_like(odd)

    flat[...] = flux_ref[0].astype(F32)
    low = lax.broadcasted_iota(jnp.int32, (surf, 128), 1) < 64
    zero = jnp.zeros((surf, 128), F32)
    for t in range(count // 2):
        here = flat[t * surf : (t + 1) * surf, :]
        there = pltpu.roll(here, 64, 1)
        even[2 * t, 0:surf, :] = jnp.where(low, here, zero)
        odd[2 * t, 0:surf, :] = jnp.where(low, zero, there)
        even[2 * t + 1, 0:surf, :] = jnp.where(low, there, zero)
        odd[2 * t + 1, 0:surf, :] = jnp.where(low, zero, here)
    for pair in range(slots // 2):
        a, b = 2 * pair, 2 * pair + 1
        to_a, to_b = dst[0, o, a], dst[0, o, b]
        to_a = jnp.where(to_a < 0, count, to_a)
        to_b = jnp.where(to_b < 0, count, to_b)
        lhs = jnp.concatenate([even[to_a], odd[to_b]], axis=0).astype(BF16)
        got = lax.dot_general(
            lhs, w_ref[0, 0, :, pair * 128 : pair * 128 + 128], (((1,), (1,)), ((), ())), preferred_element_type=F32
        )
        from_a, from_b = src[0, o, a], src[0, o, b]
        total[from_a] = total[from_a] + got[:8]
        total[from_b] = total[from_b] + got[8:]

    @pl.when(o == pl.num_programs(0) - 1)
    def _():
        for pair in range(total.shape[0] // 2):
            both = jnp.concatenate([total[2 * pair], total[2 * pair + 1]], axis=1)
            out_ref[:, pair * 128 : pair * 128 + 128] = both[:surf]


def shards(
    grp_n, dom_n, lev_n,
    atm_surface, atm_levels, margin_weights, src_block, dst_block, ice_cover, ice_flux, ocean_state, drag, level_weights,
    neighbours,
):
    surf, columns = atm_surface.shape
    levels = atm_levels.shape[0]
    near, width, across = margin_weights.shape[1:]
    cells = ice_cover.shape[0]
    tiles = cells // 128
    flat_rows = tiles * ROWS
    whole = lambda shape: pl.BlockSpec(shape, lambda o, *_: (0,) * len(shape))
    weights = pl.BlockSpec((1, 1, width, across), lambda o, *_: (0, o, 0, 0))
    agg = pl.pallas_call(
        forward_kernel,
        out_shape=jax.ShapeDtypeStruct((near, flat_rows, 128), BF16),
        grid_spec=pltpu.PrefetchScalarGridSpec(
            num_scalar_prefetch=2,
            grid=(near,),
            in_specs=[whole((surf, columns)), whole((levels, columns)), weights],
            out_specs=pl.BlockSpec((1, flat_rows, 128), lambda o, *_: (o, 0, 0)),
            scratch_shapes=[
                pltpu.VMEM((32, columns), F32),
                pltpu.VMEM((columns // width, 32, width), BF16),
                pltpu.VMEM((cells // width + 1, ROWS, 128), F32),
                pltpu.VMEM((cells // width + 1, ROWS, 128), F32),
            ],
        ),
        compiler_params=pltpu.CompilerParams(dimension_semantics=("arbitrary",), vmem_limit_bytes=32 * 2**20),
        name="pieces",
    )(src_block, dst_block, atm_surface, atm_levels, margin_weights)

    named = neighbours.T - HW
    named = jnp.where(named < 0, named + cells + 2 * HW, named)
    vmem = pl.BlockSpec(memory_space=pltpu.VMEM)
    dma = pltpu.SemaphoreType.DMA
    half = near // 2
    ocean_surface, ocean_levels, fluxes = pl.pallas_call(
        functools.partial(middle_kernel, grp_n, dom_n, lev_n),
        out_shape=[
            jax.ShapeDtypeStruct((surf, cells), F32),
            jax.ShapeDtypeStruct((levels, cells), F32),
            jax.ShapeDtypeStruct((near, tiles * surf, 128), BF16),
        ],
        in_specs=[vmem] * 5 + [pl.BlockSpec(memory_space=pltpu.SMEM), vmem],
        out_specs=[vmem] * 3,
        scratch_shapes=[
            pltpu.VMEM((half, flat_rows, 128), BF16),
            pltpu.VMEM((half - 1, flat_rows, 128), BF16),
            pltpu.VMEM((half, flat_rows, 128), BF16),
            pltpu.VMEM((32, cells), BF16),
            pltpu.VMEM((32, 2 * HW), BF16),
            pltpu.VMEM((cells + 2 * HW, cells), BF16),
            pltpu.VMEM((32, cells), F32),
            pltpu.VMEM((8, cells), F32),
            pltpu.VMEM((8, cells), F32),
            pltpu.VMEM((ROWS, 128), F32),
            pltpu.VMEM((8, cells), F32),
            pltpu.VMEM((tiles * surf, 128), F32),
            pltpu.VMEM((tiles * surf, 128), BF16),
            pltpu.VMEM((near - 1, tiles * surf, 128), BF16),
            pltpu.VMEM((1, cells), F32),
            pltpu.VMEM((max(lev_n - 1, 1), 1, cells), F32),
            dma((half,)), dma((half,)),
            dma((half,)), dma((half,)),
            dma((2,)), dma((2,)),
            dma((3,)), dma((3,)),
            dma((near - 1,)), dma((near - 1,)),
        ],
        compiler_params=pltpu.CompilerParams(collective_id=0, has_side_effects=True, vmem_limit_bytes=48 * 2**20),
        name="middle",
    )(agg, ice_cover.reshape(1, cells), ice_flux, ocean_state, drag.reshape(1, cells), level_weights, named)

    atm_flux = pl.pallas_call(
        back_kernel,
        out_shape=jax.ShapeDtypeStruct((surf, columns), F32),
        grid_spec=pltpu.PrefetchScalarGridSpec(
            num_scalar_prefetch=2,
            grid=(near,),
            in_specs=[pl.BlockSpec((1, tiles * surf, 128), lambda o, *_: (o, 0, 0)), weights],
            out_specs=whole((surf, columns)),
            scratch_shapes=[
                pltpu.VMEM((tiles * surf, 128), F32),
                pltpu.VMEM((cells // width + 1, 8, 128), F32),
                pltpu.VMEM((cells // width + 1, 8, 128), F32),
                pltpu.VMEM((columns // width, 8, width), F32),
            ],
        ),
        compiler_params=pltpu.CompilerParams(dimension_semantics=("arbitrary",), vmem_limit_bytes=32 * 2**20),
        name="back",
    )(src_block, dst_block, fluxes, margin_weights)
    return ocean_surface, ocean_levels, atm_flux


def solution(mesh):
    return jax.shard_map(
        functools.partial(shards, mesh.shape["grp"], mesh.shape["dom"], mesh.shape["lev"]),
        mesh=mesh,
        in_specs=(
            P("lev", ("grp", "dom")),
            P("lev", ("grp", "dom")),
            P(("grp", "dom"), None, None, None),
            P(("grp", "dom"), None, None),
            P(("grp", "dom"), None, None),
            P(("grp", "dom")),
            P("lev", ("grp", "dom")),
            P("lev", ("grp", "dom")),
            P(("grp", "dom")),
            P("lev"),
            P(("grp", "dom"), None),
        ),
        out_specs=(P("lev", ("grp", "dom")), P("lev", ("grp", "dom")), P("lev", ("grp", "dom"))),
        check_vma=False,
    )
```

```python
import functools

import jax
import jax.numpy as jnp
from jax import lax
from jax.experimental import pallas as pl
from jax.experimental.pallas import tpu as pltpu
from jax.sharding import PartitionSpec as P

HW = 128
KAPPA = 0.5
ROWS = 24
MESH = pl.DeviceIdType.MESH
F32 = jnp.float32
BF16 = jnp.bfloat16


def dot(a, b):
    return jnp.dot(a, b, preferred_element_type=F32)


def forward_kernel(src_hbm, dst_hbm, surf_hbm, lev_hbm, w_hbm, out_ref, src, dst, surf_ref, lev_ref, w_ref, joint, blocks, even, odd, small, big):
    levels, surf = lev_ref.shape[0], surf_ref.shape[0]
    near, width, across = w_ref.shape
    slots = across // width
    count = even.shape[0] - 1
    arriving = [
        pltpu.make_async_copy(here, there, small.at[n])
        for n, (here, there) in enumerate([(lev_hbm, lev_ref), (surf_hbm, surf_ref), (src_hbm.at[0], src), (dst_hbm.at[0], dst)])
    ]
    weights = [pltpu.make_async_copy(w_hbm.at[0, o], w_ref.at[o], big.at[o]) for o in range(near)]
    for one in arriving + weights:
        one.start()
    joint[levels + surf :, :] = jnp.zeros_like(joint[levels + surf :, :])
    arriving[0].wait()
    arriving[1].wait()
    joint[0:levels, :] = lev_ref[...].astype(F32)
    joint[levels : levels + surf, :] = surf_ref[...].astype(F32)
    for pair in range(blocks.shape[0] // 2):
        both = joint[:, pair * 128 : pair * 128 + 128].astype(BF16)
        blocks[2 * pair] = both[:, :64]
        blocks[2 * pair + 1] = both[:, 64:]
    arriving[2].wait()
    arriving[3].wait()
    low = lax.broadcasted_iota(jnp.int32, (ROWS, 128), 1) < 64

    def offset(o, carry):
        pltpu.make_async_copy(w_hbm.at[0, o], w_ref.at[o], big.at[o]).wait()
        even[...] = jnp.zeros_like(even)
        odd[...] = jnp.zeros_like(odd)
        for pair in range(slots // 2):
            a, b = 2 * pair, 2 * pair + 1
            lhs = jnp.concatenate([blocks[src[o, a]], blocks[src[o, b]]], axis=0)
            got = dot(lhs, w_ref[o, :, pair * 128 : pair * 128 + 128]).astype(BF16).astype(F32)
            to_a, to_b = dst[o, a], dst[o, b]
            to_a = jnp.where(to_a < 0, count, to_a)
            to_b = jnp.where(to_b < 0, count, to_b)
            even[to_a] = even[to_a] + got[:ROWS]
            odd[to_b] = odd[to_b] + got[32 : 32 + ROWS]

        def joined(t):
            left = even[2 * t] + pltpu.roll(odd[2 * t], 64, 1)
            right = pltpu.roll(even[2 * t + 1], 64, 1) + odd[2 * t + 1]
            return jnp.where(low, left, right)

        for t in range(0, count // 2, 2):
            both = jnp.concatenate([joined(t), joined(t + 1)], axis=0)
            out_ref[o, t * ROWS : (t + 2) * ROWS, :] = both.astype(BF16)
        return carry

    lax.fori_loop(0, near, offset, 0)


def middle_kernel(
    grp_n, dom_n, lev_n,
    agg, ice_cover, ice_flux, ocean_state, drag, level_weights, neighbours,
    surf_out, lev_out, flux_out,
    sib, comb, recv, own, halo, named, hits, counts, around, ice8, state8, lw_rows, surf8, flat, flux_send, flux_recv, col_send, col_recv,
    sib_s, sib_r, far_s, far_r, halo_s, halo_r, col_s, col_r, flux_s, flux_r,
):
    grp, dom, lev = lax.axis_index("grp"), lax.axis_index("dom"), lax.axis_index("lev")
    parts = grp_n * dom_n
    p = grp * dom_n + dom
    core = lax.rem(dom, 2)
    levels, surf = lev_out.shape[0], surf_out.shape[0]
    cells = lev_out.shape[1]
    tiles = cells // 128
    near = agg.shape[0]

    def part(by):
        q = lax.rem(p + by + parts, parts)
        return (q // dom_n, lax.rem(q, dom_n), lev)

    def ring(by):
        return (grp, lax.rem(dom + by + dom_n, dom_n), lev)

    def column_peer(by):
        return (grp, dom, lax.rem(lev + by, lev_n))

    sibling = (grp, dom + 1 - 2 * core, lev)

    barrier = pltpu.get_barrier_semaphore()
    greeted = 0
    for by in range(1, near + 1):
        for sign in (1, -1):
            pl.semaphore_signal(barrier, inc=1, device_id=part(sign * by), device_id_type=MESH)
            greeted += 1
    for by in (1, -1):
        pl.semaphore_signal(barrier, inc=1, device_id=ring(by), device_id_type=MESH)
        greeted += 1
    for by in range(1, lev_n):
        pl.semaphore_signal(barrier, inc=1, device_id=column_peer(by), device_id_type=MESH)
        greeted += 1
    pl.semaphore_wait(barrier, greeted)

    def copy(src, dst, send, got, device):
        return pltpu.make_async_remote_copy(
            src_ref=src, dst_ref=dst, send_sem=send, recv_sem=got, device_id=device, device_id_type=MESH
        )

    sib_copies = [copy(agg.at[2 * m + 1], sib.at[m], sib_s.at[m], sib_r.at[m], sibling) for m in range(3)]
    sib_copies.append(copy(agg.at[7], sib.at[3], sib_s.at[3], sib_r.at[3], part(1)))
    far1 = copy(comb.at[0], recv.at[0], far_s.at[0], far_r.at[0], part(2))
    far2 = copy(comb.at[1], recv.at[1], far_s.at[1], far_r.at[1], part(4))
    far3 = copy(comb.at[2], recv.at[2], far_s.at[2], far_r.at[2], part(2))
    for m in reversed(range(4)):
        sib_copies[m].start()

    def wide(ref, n):
        return ref[n].astype(F32)

    sib_copies[3].wait_recv()
    sib_copies[2].wait_recv()
    comb[2] = (wide(agg, 6) + wide(sib, 3) + jnp.where(core == 0, wide(sib, 2), 0.0)).astype(BF16)
    far3.start()
    sib_copies[1].wait_recv()
    sib_copies[0].wait_recv()
    comb[0] = (wide(agg, 2) + wide(sib, core)).astype(BF16)
    far1.start()

    nb = named.shape[0]
    ext_tiles = counts.shape[0] // 128
    place = neighbours[...] - HW
    named[...] = jnp.where(place < 0, place + cells + 2 * HW, place)

    def hit_rows(h, carry):
        for e in range(nb):
            hit = jnp.where(jnp.broadcast_to(named[e : e + 1, :] // 128, (16, cells)) == h, 1.0, 0.0)
            hits[e, pl.ds(pl.multiple_of(h * 16, 16), 16), :] = hit.astype(BF16)
        return carry

    def count_cells(n, carry):
        lanes = pl.ds(pl.multiple_of(n * 128, 128), 128)
        rows = [jnp.broadcast_to(named[e : e + 1, lanes] % 128, (16, 128)) for e in range(nb)]

        def block(lb, carry):
            row = lax.broadcasted_iota(jnp.int32, (16, 128), 0) + lb * 16
            spots = [jnp.where(rows[e] == row, 1.0, 0.0).astype(BF16) for e in range(nb)]
            for h in range(ext_tiles):
                total = spots[0] * hits[0, h * 16 : h * 16 + 16, lanes]
                for e in range(1, nb):
                    total = total + spots[e] * hits[e, h * 16 : h * 16 + 16, lanes]
                counts[pl.ds(pl.multiple_of(h * 128 + lb * 16, 16), 16), lanes] = total
            return carry

        return lax.fori_loop(0, 8, block, carry)

    lax.fori_loop(0, ext_tiles, hit_rows, 0)
    far3.wait_recv()
    comb[1] = (wide(agg, 4) + wide(sib, 1 + core) + wide(recv, 2)).astype(BF16)
    far2.start()
    lax.fori_loop(0, tiles, count_cells, 0)

    first = levels - 16
    ice8[...] = jnp.zeros_like(ice8)
    state8[...] = jnp.zeros_like(state8)
    ice8[first : first + surf, :] = ice_flux[...].astype(F32)
    state8[first : first + surf, :] = ocean_state[...].astype(F32)
    lw_rows[...] = jnp.zeros_like(lw_rows)
    for k in range(levels):
        lw_rows[k : k + 1, :] = jnp.full((1, 128), level_weights[k], F32)

    far1.wait_recv()
    far2.wait_recv()

    is_surf = lax.broadcasted_iota(jnp.int32, (8, 128), 0) >= first
    for t in range(0, tiles, 2):
        rows = slice(t * ROWS, (t + 2) * ROWS)
        total = agg[0, rows, :].astype(F32) + recv[0, rows, :].astype(F32) + recv[1, rows, :].astype(F32)
        total = total + jnp.where(core == 1, sib[0, rows, :].astype(F32), 0.0)
        for u in range(2):
            lanes = slice((t + u) * 128, (t + u + 1) * 128)
            one = total[u * ROWS : (u + 1) * ROWS]
            share = ice_cover[:, lanes]
            tail = jnp.where(is_surf, (1.0 - share) * one[16:] + share * ice8[:, lanes], one[16:])
            own[:, lanes] = jnp.concatenate([one[:16], tail, jnp.zeros((8, 128), F32)], axis=0).astype(BF16)

    to_prev = copy(own.at[:, 0:HW], halo.at[:, 0:HW], halo_s.at[0], halo_r.at[0], ring(-1))
    to_next = copy(own.at[:, cells - HW : cells], halo.at[:, HW : 2 * HW], halo_s.at[1], halo_r.at[1], ring(1))
    to_prev.start()
    to_next.start()
    for c in range(cells // 256):
        lanes = slice(c * 256, c * 256 + 256)
        around[:, lanes] = dot(own[...], counts[0:cells, lanes])
    to_prev.wait_recv()
    to_next.wait_recv()
    for c in range(cells // 256):
        lanes = slice(c * 256, c * 256 + 256)
        total = around[:, lanes] + dot(halo[...], counts[cells : cells + 2 * HW, lanes])
        forcing = (1.0 - KAPPA) * own[:, lanes].astype(F32) + (KAPPA / named.shape[0]) * total
        forcing = forcing[:ROWS]
        lev_out[:, lanes] = forcing[:levels]
        surf_out[:, lanes] = forcing[levels : levels + surf]
        surf8[:, lanes] = forcing[16:]
        weight = jnp.concatenate([lw_rows[...], lw_rows[...]], axis=1)
        col_send[:, lanes] = jnp.sum(weight * forcing, axis=0, keepdims=True)

    col_copies = [copy(col_send, col_recv.at[by - 1], col_s.at[by - 1], col_r.at[by - 1], column_peer(by)) for by in range(1, lev_n)]
    for one in col_copies:
        one.start()
    for one in col_copies:
        one.wait_recv()
    column = col_send[...]
    for by in range(1, lev_n):
        column = column + col_recv[by - 1]
    flux = drag[...] * (state8[...] - surf8[...] + column)
    for t in range(tiles):
        flat[t * surf : (t + 1) * surf, :] = flux[first : first + surf, t * 128 : t * 128 + 128]
    flux_send[...] = flat[...].astype(BF16)
    flux_copies = [copy(flux_send, flux_recv.at[o - 1], flux_s.at[o - 1], flux_r.at[o - 1], part(-o)) for o in range(1, near)]
    for one in reversed(flux_copies):
        one.start()
    flux_out[0] = flux_send[...]
    for o in range(1, near):
        flux_copies[o - 1].wait_recv()
        flux_out[o] = flux_recv[o - 1]

    for one in sib_copies + [far1, far2, far3, to_prev, to_next] + col_copies + flux_copies:
        one.wait_send()


def back_kernel(src_hbm, dst_hbm, flux_ref, w_ref, surf_ref, lev_ref, out_ref, surf_out, lev_out, src, dst, flat, even, odd, total, sems):
    surf = out_ref.shape[0]
    near, width, across = w_ref.shape[1:]
    slots = across // width
    count = even.shape[0] // near - 1
    copies = [
        pltpu.make_async_copy(here, there, sems.at[n])
        for n, (here, there) in enumerate([(src_hbm.at[0], src), (dst_hbm.at[0], dst), (surf_ref, surf_out), (lev_ref, lev_out)])
    ]
    for one in copies:
        one.start()
    total[...] = jnp.zeros_like(total)
    even[...] = jnp.zeros_like(even)
    odd[...] = jnp.zeros_like(odd)
    low = lax.broadcasted_iota(jnp.int32, (surf, 128), 1) < 64
    zero = jnp.zeros((surf, 128), F32)
    flat[...] = flux_ref[...].astype(F32)

    def spread(o, carry):
        base = o * (count + 1)
        for t in range(count // 2):
            here = flat[o, t * surf : (t + 1) * surf, :]
            there = pltpu.roll(here, 64, 1)
            even[base + 2 * t, 0:surf, :] = jnp.where(low, here, zero)
            odd[base + 2 * t, 0:surf, :] = jnp.where(low, zero, there)
            even[base + 2 * t + 1, 0:surf, :] = jnp.where(low, there, zero)
            odd[base + 2 * t + 1, 0:surf, :] = jnp.where(low, zero, here)
        return carry

    lax.fori_loop(0, near, spread, 0)
    copies[0].wait()
    copies[1].wait()

    def offset(o, carry):
        base = o * (count + 1)
        for pair in range(slots // 2):
            a, b = 2 * pair, 2 * pair + 1
            to_a, to_b = dst[o, a], dst[o, b]
            to_a = jnp.where(to_a < 0, count, to_a)
            to_b = jnp.where(to_b < 0, count, to_b)
            lhs = jnp.concatenate([even[base + to_a], odd[base + to_b]], axis=0).astype(BF16)
            got = lax.dot_general(
                lhs, w_ref[0, o, :, pair * 128 : pair * 128 + 128], (((1,), (1,)), ((), ())), preferred_element_type=F32
            )
            from_a, from_b = src[o, a], src[o, b]
            total[from_a] = total[from_a] + got[:8]
            total[from_b] = total[from_b] + got[8:]
        return carry

    lax.fori_loop(0, near, offset, 0)
    for pair in range(total.shape[0] // 2):
        both = jnp.concatenate([total[2 * pair], total[2 * pair + 1]], axis=1)
        out_ref[:, pair * 128 : pair * 128 + 128] = both[:surf]
    copies[2].wait()
    copies[3].wait()


def shards(
    grp_n, dom_n, lev_n,
    atm_surface, atm_levels, margin_weights, src_block, dst_block, ice_cover, ice_flux, ocean_state, drag, level_weights,
    neighbours,
):
    surf, columns = atm_surface.shape
    levels = atm_levels.shape[0]
    near, width, across = margin_weights.shape[1:]
    cells = ice_cover.shape[0]
    tiles = cells // 128
    flat_rows = tiles * ROWS
    hbm = pl.BlockSpec(memory_space=pltpu.HBM)
    dma = pltpu.SemaphoreType.DMA
    agg = pl.pallas_call(
        forward_kernel,
        out_shape=jax.ShapeDtypeStruct((near, flat_rows, 128), BF16),
        in_specs=[hbm] * 5,
        out_specs=pl.BlockSpec(memory_space=pltpu.VMEM),
        scratch_shapes=[
            pltpu.SMEM(src_block.shape[1:], jnp.int32),
            pltpu.SMEM(src_block.shape[1:], jnp.int32),
            pltpu.VMEM((surf, columns), BF16),
            pltpu.VMEM((levels, columns), BF16),
            pltpu.VMEM((near, width, across), BF16),
            pltpu.VMEM((32, columns), F32),
            pltpu.VMEM((columns // width, 32, width), BF16),
            pltpu.VMEM((cells // width + 1, ROWS, 128), F32),
            pltpu.VMEM((cells // width + 1, ROWS, 128), F32),
            dma((4,)),
            dma((near,)),
        ],
        compiler_params=pltpu.CompilerParams(vmem_limit_bytes=32 * 2**20),
        name="pieces",
    )(*[pltpu.with_memory_space_constraint(x, pltpu.HBM) for x in (src_block, dst_block, atm_surface, atm_levels, margin_weights)])

    vmem = pl.BlockSpec(memory_space=pltpu.VMEM)
    ocean_surface, ocean_levels, fluxes = pl.pallas_call(
        functools.partial(middle_kernel, grp_n, dom_n, lev_n),
        out_shape=[
            jax.ShapeDtypeStruct((surf, cells), F32),
            jax.ShapeDtypeStruct((levels, cells), F32),
            jax.ShapeDtypeStruct((near, tiles * surf, 128), BF16),
        ],
        in_specs=[vmem] * 5 + [pl.BlockSpec(memory_space=pltpu.SMEM), vmem],
        out_specs=[vmem] * 3,
        scratch_shapes=[
            pltpu.VMEM((4, flat_rows, 128), BF16),
            pltpu.VMEM((3, flat_rows, 128), BF16),
            pltpu.VMEM((3, flat_rows, 128), BF16),
            pltpu.VMEM((32, cells), BF16),
            pltpu.VMEM((32, 2 * HW), BF16),
            pltpu.VMEM((neighbours.shape[1], cells), jnp.int32),
            pltpu.VMEM((neighbours.shape[1], (cells + 2 * HW) // 8, cells), BF16),
            pltpu.VMEM((cells + 2 * HW, cells), BF16),
            pltpu.VMEM((32, cells), F32),
            pltpu.VMEM((8, cells), F32),
            pltpu.VMEM((8, cells), F32),
            pltpu.VMEM((ROWS, 128), F32),
            pltpu.VMEM((8, cells), F32),
            pltpu.VMEM((tiles * surf, 128), F32),
            pltpu.VMEM((tiles * surf, 128), BF16),
            pltpu.VMEM((near - 1, tiles * surf, 128), BF16),
            pltpu.VMEM((1, cells), F32),
            pltpu.VMEM((max(lev_n - 1, 1), 1, cells), F32),
            dma((4,)), dma((4,)),
            dma((3,)), dma((3,)),
            dma((2,)), dma((2,)),
            dma((3,)), dma((3,)),
            dma((near - 1,)), dma((near - 1,)),
        ],
        compiler_params=pltpu.CompilerParams(collective_id=0, has_side_effects=True, vmem_limit_bytes=48 * 2**20),
        name="middle",
    )(agg, ice_cover.reshape(1, cells), ice_flux, ocean_state, drag.reshape(1, cells), level_weights, neighbours.T)

    atm_flux, ocean_surface, ocean_levels = pl.pallas_call(
        back_kernel,
        out_shape=[
            jax.ShapeDtypeStruct((surf, columns), F32),
            jax.ShapeDtypeStruct((surf, cells), F32),
            jax.ShapeDtypeStruct((levels, cells), F32),
        ],
        in_specs=[hbm] * 2 + [vmem] * 4,
        out_specs=[vmem, hbm, hbm],
        scratch_shapes=[
            pltpu.SMEM(src_block.shape[1:], jnp.int32),
            pltpu.SMEM(src_block.shape[1:], jnp.int32),
            pltpu.VMEM((near, tiles * surf, 128), F32),
            pltpu.VMEM((near * (cells // width + 1), 8, 128), F32),
            pltpu.VMEM((near * (cells // width + 1), 8, 128), F32),
            pltpu.VMEM((columns // width, 8, width), F32),
            dma((4,)),
        ],
        compiler_params=pltpu.CompilerParams(vmem_limit_bytes=32 * 2**20),
        name="back",
    )(src_block, dst_block, fluxes, margin_weights, ocean_surface, ocean_levels)
    return ocean_surface, ocean_levels, atm_flux


def solution(mesh):
    return jax.shard_map(
        functools.partial(shards, mesh.shape["grp"], mesh.shape["dom"], mesh.shape["lev"]),
        mesh=mesh,
        in_specs=(
            P("lev", ("grp", "dom")),
            P("lev", ("grp", "dom")),
            P(("grp", "dom"), None, None, None),
            P(("grp", "dom"), None, None),
            P(("grp", "dom"), None, None),
            P(("grp", "dom")),
            P("lev", ("grp", "dom")),
            P("lev", ("grp", "dom")),
            P(("grp", "dom")),
            P("lev"),
            P(("grp", "dom"), None),
        ),
        out_specs=(P("lev", ("grp", "dom")), P("lev", ("grp", "dom")), P("lev", ("grp", "dom"))),
        check_vma=False,
    )
```

```python
import functools

import jax
import jax.numpy as jnp
from jax import lax
from jax.experimental import pallas as pl
from jax.experimental.pallas import tpu as pltpu
from jax.sharding import PartitionSpec as P

HW = 128
KAPPA = 0.5
ROWS = 24
MESH = pl.DeviceIdType.MESH
F32 = jnp.float32
BF16 = jnp.bfloat16


def dot(a, b):
    return jnp.dot(a, b, preferred_element_type=F32)


def forward_kernel(src_hbm, dst_hbm, surf_hbm, lev_hbm, w_hbm, out_ref, src, dst, surf_ref, lev_ref, w_ref, joint, blocks, even, odd, small, big):
    levels, surf = lev_ref.shape[0], surf_ref.shape[0]
    near, width, across = w_ref.shape
    slots = across // width
    count = even.shape[0] - 1
    arriving = [
        pltpu.make_async_copy(here, there, small.at[n])
        for n, (here, there) in enumerate([(lev_hbm, lev_ref), (surf_hbm, surf_ref), (src_hbm.at[0], src), (dst_hbm.at[0], dst)])
    ]
    weights = [pltpu.make_async_copy(w_hbm.at[0, o], w_ref.at[o], big.at[o]) for o in range(near)]
    for one in arriving + weights:
        one.start()
    joint[levels + surf :, :] = jnp.zeros_like(joint[levels + surf :, :])
    arriving[0].wait()
    arriving[1].wait()
    joint[0:levels, :] = lev_ref[...].astype(F32)
    joint[levels : levels + surf, :] = surf_ref[...].astype(F32)
    for pair in range(blocks.shape[0] // 2):
        both = joint[:, pair * 128 : pair * 128 + 128].astype(BF16)
        blocks[2 * pair] = both[:, :64]
        blocks[2 * pair + 1] = both[:, 64:]
    arriving[2].wait()
    arriving[3].wait()
    low = lax.broadcasted_iota(jnp.int32, (ROWS, 128), 1) < 64

    def offset(o, carry):
        pltpu.make_async_copy(w_hbm.at[0, o], w_ref.at[o], big.at[o]).wait()
        even[...] = jnp.zeros_like(even)
        odd[...] = jnp.zeros_like(odd)
        for pair in range(slots // 2):
            a, b = 2 * pair, 2 * pair + 1
            lhs = jnp.concatenate([blocks[src[o, a]], blocks[src[o, b]]], axis=0)
            got = dot(lhs, w_ref[o, :, pair * 128 : pair * 128 + 128]).astype(BF16).astype(F32)
            to_a, to_b = dst[o, a], dst[o, b]
            to_a = jnp.where(to_a < 0, count, to_a)
            to_b = jnp.where(to_b < 0, count, to_b)
            even[to_a] = even[to_a] + got[:ROWS]
            odd[to_b] = odd[to_b] + got[32 : 32 + ROWS]

        def joined(t):
            left = even[2 * t] + pltpu.roll(odd[2 * t], 64, 1)
            right = pltpu.roll(even[2 * t + 1], 64, 1) + odd[2 * t + 1]
            return jnp.where(low, left, right)

        for t in range(0, count // 2, 2):
            both = jnp.concatenate([joined(t), joined(t + 1)], axis=0)
            out_ref[o, t * ROWS : (t + 2) * ROWS, :] = both.astype(BF16)
        return carry

    lax.fori_loop(0, near, offset, 0)


def middle_kernel(
    grp_n, dom_n, lev_n,
    agg, ice_cover, ice_flux, ocean_state, drag, level_weights, neighbours,
    surf_out, lev_out, flux_out,
    sib, comb, recv, own, halo, tile_of, place_of, counts, around, ice8, state8, lw_rows, flat, flux_send, flux_recv, col_send, col_recv,
    sib_s, sib_r, far_s, far_r, halo_s, halo_r, col_s, col_r, flux_s, flux_r,
):
    grp, dom, lev = lax.axis_index("grp"), lax.axis_index("dom"), lax.axis_index("lev")
    parts = grp_n * dom_n
    p = grp * dom_n + dom
    core = lax.rem(dom, 2)
    levels, surf = lev_out.shape[0], surf_out.shape[0]
    cells = lev_out.shape[1]
    tiles = cells // 128
    near = agg.shape[0]

    def part(by):
        q = lax.rem(p + by + parts, parts)
        return (q // dom_n, lax.rem(q, dom_n), lev)

    def ring(by):
        return (grp, lax.rem(dom + by + dom_n, dom_n), lev)

    def column_peer(by):
        return (grp, dom, lax.rem(lev + by, lev_n))

    sibling = (grp, dom + 1 - 2 * core, lev)

    barrier = pltpu.get_barrier_semaphore()
    greeted = 0
    for by in range(1, near):
        for sign in (1, -1):
            pl.semaphore_signal(barrier, inc=1, device_id=part(sign * by), device_id_type=MESH)
            greeted += 1
    for by in (1, -1):
        pl.semaphore_signal(barrier, inc=1, device_id=ring(by), device_id_type=MESH)
        greeted += 1
    for by in range(1, lev_n):
        pl.semaphore_signal(barrier, inc=1, device_id=column_peer(by), device_id_type=MESH)
        greeted += 1
    first = levels - 16
    ice8[...] = jnp.zeros_like(ice8)
    state8[...] = jnp.zeros_like(state8)
    ice8[first : first + surf, :] = ice_flux[...].astype(F32)
    state8[first : first + surf, :] = ocean_state[...].astype(F32)
    lw_rows[...] = jnp.zeros_like(lw_rows)
    for k in range(levels):
        lw_rows[k : k + 1, :] = jnp.full((1, 128), level_weights[k], F32)
    nb = neighbours.shape[0]
    place = neighbours[...] - HW
    place = jnp.where(place < 0, place + cells + 2 * HW, place)
    tile_of[...] = place >> 7
    place_of[...] = place & 127
    pl.semaphore_wait(barrier, greeted)

    def copy(src, dst, send, got, device):
        return pltpu.make_async_remote_copy(
            src_ref=src, dst_ref=dst, send_sem=send, recv_sem=got, device_id=device, device_id_type=MESH
        )

    sib_copies = [copy(agg.at[2 * m + 1], sib.at[m], sib_s.at[m], sib_r.at[m], sibling) for m in range(3)]
    sib_copies.append(copy(agg.at[7], sib.at[3], sib_s.at[3], sib_r.at[3], part(1)))
    far1 = copy(comb.at[0], recv.at[0], far_s.at[0], far_r.at[0], part(2))
    far2 = copy(comb.at[1], recv.at[1], far_s.at[1], far_r.at[1], part(4))
    far3 = copy(comb.at[2], recv.at[2], far_s.at[2], far_r.at[2], part(2))
    for m in reversed(range(4)):
        sib_copies[m].start()

    def wide(ref, n):
        return ref[n].astype(F32)

    sib_copies[3].wait_recv()
    sib_copies[2].wait_recv()
    comb[2] = (wide(agg, 6) + wide(sib, 3) + jnp.where(core == 0, wide(sib, 2), 0.0)).astype(BF16)
    far3.start()
    sib_copies[1].wait_recv()
    sib_copies[0].wait_recv()
    comb[0] = (wide(agg, 2) + wide(sib, core)).astype(BF16)
    far1.start()

    def count_cells(n, carry):
        lanes = pl.ds(pl.multiple_of(n * 128, 128), 128)
        row = lax.broadcasted_iota(jnp.int32, (128, 128), 0)
        spots, tile_rows = [], []
        for e in range(nb):
            spot = jnp.where(jnp.broadcast_to(place_of[e : e + 1, lanes], (128, 128)) == row, 1.0, 0.0)
            spots.append(spot.astype(BF16))
            tile_rows.append(jnp.broadcast_to(tile_of[e : e + 1, lanes], (16, 128)).astype(F32).astype(BF16))
        for h in range(counts.shape[0] // 128):
            total = None
            for e in range(nb):
                hit = tile_rows[e] == jnp.full((16, 128), h, BF16)
                term = jnp.where(jnp.concatenate([hit] * 8, axis=0), spots[e], jnp.zeros_like(spots[e]))
                total = term if total is None else total + term
            counts[h * 128 : h * 128 + 128, lanes] = total
        return carry

    early = 3 * tiles // 8
    lax.fori_loop(0, early, count_cells, 0)
    far3.wait_recv()
    comb[1] = (wide(agg, 4) + wide(sib, 1 + core) + wide(recv, 2)).astype(BF16)
    far2.start()
    lax.fori_loop(early, tiles, count_cells, 0)

    far1.wait_recv()
    far2.wait_recv()

    is_surf = lax.broadcasted_iota(jnp.int32, (8, 128), 0) >= first
    for t in range(0, tiles, 2):
        rows = slice(t * ROWS, (t + 2) * ROWS)
        total = agg[0, rows, :].astype(F32) + recv[0, rows, :].astype(F32) + recv[1, rows, :].astype(F32)
        total = total + jnp.where(core == 1, sib[0, rows, :].astype(F32), 0.0)
        for u in range(2):
            lanes = slice((t + u) * 128, (t + u + 1) * 128)
            one = total[u * ROWS : (u + 1) * ROWS]
            share = ice_cover[:, lanes]
            tail = jnp.where(is_surf, (1.0 - share) * one[16:] + share * ice8[:, lanes], one[16:])
            own[:, lanes] = jnp.concatenate([one[:16], tail, jnp.zeros((8, 128), F32)], axis=0).astype(BF16)

    to_prev = copy(own.at[:, 0:HW], halo.at[:, 0:HW], halo_s.at[0], halo_r.at[0], ring(-1))
    to_next = copy(own.at[:, cells - HW : cells], halo.at[:, HW : 2 * HW], halo_s.at[1], halo_r.at[1], ring(1))
    to_prev.start()
    to_next.start()
    for c in range(cells // 256):
        lanes = slice(c * 256, c * 256 + 256)
        around[:, lanes] = dot(own[...], counts[0:cells, lanes])
    to_prev.wait_recv()
    to_next.wait_recv()
    weight = jnp.concatenate([lw_rows[...], lw_rows[...]], axis=1)
    for c in range(cells // 256):
        lanes = slice(c * 256, c * 256 + 256)
        total = around[:, lanes] + dot(halo[...], counts[cells : cells + 2 * HW, lanes])
        forcing = (1.0 - KAPPA) * own[:, lanes].astype(F32) + (KAPPA / nb) * total
        around[:, lanes] = forcing
        col_send[:, lanes] = jnp.sum(weight * forcing[:ROWS], axis=0, keepdims=True)

    col_copies = [copy(col_send, col_recv.at[by - 1], col_s.at[by - 1], col_r.at[by - 1], column_peer(by)) for by in range(1, lev_n)]
    for one in col_copies:
        one.start()
    lev_out[...] = around[:levels, :]
    surf_out[...] = around[levels : levels + surf, :]
    for one in col_copies:
        one.wait_recv()
    column = col_send[...]
    for by in range(1, lev_n):
        column = column + col_recv[by - 1]
    flux = drag[...] * (state8[...] - around[16:ROWS, :] + column)
    for t in range(tiles):
        flat[t * surf : (t + 1) * surf, :] = flux[first : first + surf, t * 128 : t * 128 + 128]
    flux_send[...] = flat[...].astype(BF16)
    flux_copies = [copy(flux_send, flux_recv.at[o - 1], flux_s.at[o - 1], flux_r.at[o - 1], part(-o)) for o in range(1, near)]
    for one in reversed(flux_copies):
        one.start()
    flux_out[0] = flux_send[...]
    for o in range(1, near):
        flux_copies[o - 1].wait_recv()
        flux_out[o] = flux_recv[o - 1]

    for one in sib_copies + [far1, far2, far3, to_prev, to_next] + col_copies + flux_copies:
        one.wait_send()


def back_kernel(src_hbm, dst_hbm, flux_ref, w_ref, surf_ref, lev_ref, out_ref, surf_out, lev_out, src, dst, flat, even, odd, total, sems):
    surf = out_ref.shape[0]
    near, width, across = w_ref.shape[1:]
    slots = across // width
    count = even.shape[0] // near - 1
    copies = [
        pltpu.make_async_copy(here, there, sems.at[n])
        for n, (here, there) in enumerate([(src_hbm.at[0], src), (dst_hbm.at[0], dst), (surf_ref, surf_out), (lev_ref, lev_out)])
    ]
    for one in copies:
        one.start()
    total[...] = jnp.zeros_like(total)
    even[...] = jnp.zeros_like(even)
    odd[...] = jnp.zeros_like(odd)
    low = lax.broadcasted_iota(jnp.int32, (surf, 128), 1) < 64
    zero = jnp.zeros((surf, 128), F32)
    flat[...] = flux_ref[...].astype(F32)

    def spread(o, carry):
        base = o * (count + 1)
        for t in range(count // 2):
            here = flat[o, t * surf : (t + 1) * surf, :]
            there = pltpu.roll(here, 64, 1)
            even[base + 2 * t, 0:surf, :] = jnp.where(low, here, zero)
            odd[base + 2 * t, 0:surf, :] = jnp.where(low, zero, there)
            even[base + 2 * t + 1, 0:surf, :] = jnp.where(low, there, zero)
            odd[base + 2 * t + 1, 0:surf, :] = jnp.where(low, zero, here)
        return carry

    lax.fori_loop(0, near, spread, 0)
    copies[0].wait()
    copies[1].wait()

    def offset(o, carry):
        base = o * (count + 1)
        for pair in range(slots // 2):
            a, b = 2 * pair, 2 * pair + 1
            to_a, to_b = dst[o, a], dst[o, b]
            to_a = jnp.where(to_a < 0, count, to_a)
            to_b = jnp.where(to_b < 0, count, to_b)
            lhs = jnp.concatenate([even[base + to_a], odd[base + to_b]], axis=0).astype(BF16)
            got = lax.dot_general(
                lhs, w_ref[0, o, :, pair * 128 : pair * 128 + 128], (((1,), (1,)), ((), ())), preferred_element_type=F32
            )
            from_a, from_b = src[o, a], src[o, b]
            total[from_a] = total[from_a] + got[:8]
            total[from_b] = total[from_b] + got[8:]
        return carry

    lax.fori_loop(0, near, offset, 0)
    for pair in range(total.shape[0] // 2):
        both = jnp.concatenate([total[2 * pair], total[2 * pair + 1]], axis=1)
        out_ref[:, pair * 128 : pair * 128 + 128] = both[:surf]
    copies[2].wait()
    copies[3].wait()


def shards(
    grp_n, dom_n, lev_n,
    atm_surface, atm_levels, margin_weights, src_block, dst_block, ice_cover, ice_flux, ocean_state, drag, level_weights,
    neighbours,
):
    surf, columns = atm_surface.shape
    levels = atm_levels.shape[0]
    near, width, across = margin_weights.shape[1:]
    cells = ice_cover.shape[0]
    tiles = cells // 128
    flat_rows = tiles * ROWS
    hbm = pl.BlockSpec(memory_space=pltpu.HBM)
    dma = pltpu.SemaphoreType.DMA
    agg = pl.pallas_call(
        forward_kernel,
        out_shape=jax.ShapeDtypeStruct((near, flat_rows, 128), BF16),
        in_specs=[hbm] * 5,
        out_specs=pl.BlockSpec(memory_space=pltpu.VMEM),
        scratch_shapes=[
            pltpu.SMEM(src_block.shape[1:], jnp.int32),
            pltpu.SMEM(src_block.shape[1:], jnp.int32),
            pltpu.VMEM((surf, columns), BF16),
            pltpu.VMEM((levels, columns), BF16),
            pltpu.VMEM((near, width, across), BF16),
            pltpu.VMEM((32, columns), F32),
            pltpu.VMEM((columns // width, 32, width), BF16),
            pltpu.VMEM((cells // width + 1, ROWS, 128), F32),
            pltpu.VMEM((cells // width + 1, ROWS, 128), F32),
            dma((4,)),
            dma((near,)),
        ],
        compiler_params=pltpu.CompilerParams(vmem_limit_bytes=32 * 2**20),
        name="pieces",
    )(*[pltpu.with_memory_space_constraint(x, pltpu.HBM) for x in (src_block, dst_block, atm_surface, atm_levels, margin_weights)])

    vmem = pl.BlockSpec(memory_space=pltpu.VMEM)
    ocean_surface, ocean_levels, fluxes = pl.pallas_call(
        functools.partial(middle_kernel, grp_n, dom_n, lev_n),
        out_shape=[
            jax.ShapeDtypeStruct((surf, cells), F32),
            jax.ShapeDtypeStruct((levels, cells), F32),
            jax.ShapeDtypeStruct((near, tiles * surf, 128), BF16),
        ],
        in_specs=[vmem] * 5 + [pl.BlockSpec(memory_space=pltpu.SMEM), vmem],
        out_specs=[vmem] * 3,
        scratch_shapes=[
            pltpu.VMEM((4, flat_rows, 128), BF16),
            pltpu.VMEM((3, flat_rows, 128), BF16),
            pltpu.VMEM((3, flat_rows, 128), BF16),
            pltpu.VMEM((32, cells), BF16),
            pltpu.VMEM((32, 2 * HW), BF16),
            pltpu.VMEM((neighbours.shape[1], cells), jnp.int32),
            pltpu.VMEM((neighbours.shape[1], cells), jnp.int32),
            pltpu.VMEM((cells + 2 * HW, cells), BF16),
            pltpu.VMEM((32, cells), F32),
            pltpu.VMEM((8, cells), F32),
            pltpu.VMEM((8, cells), F32),
            pltpu.VMEM((ROWS, 128), F32),
            pltpu.VMEM((tiles * surf, 128), F32),
            pltpu.VMEM((tiles * surf, 128), BF16),
            pltpu.VMEM((near - 1, tiles * surf, 128), BF16),
            pltpu.VMEM((1, cells), F32),
            pltpu.VMEM((max(lev_n - 1, 1), 1, cells), F32),
            dma((4,)), dma((4,)),
            dma((3,)), dma((3,)),
            dma((2,)), dma((2,)),
            dma((3,)), dma((3,)),
            dma((near - 1,)), dma((near - 1,)),
        ],
        compiler_params=pltpu.CompilerParams(collective_id=0, has_side_effects=True, vmem_limit_bytes=48 * 2**20),
        name="middle",
    )(agg, ice_cover.reshape(1, cells), ice_flux, ocean_state, drag.reshape(1, cells), level_weights, neighbours.T)

    atm_flux, ocean_surface, ocean_levels = pl.pallas_call(
        back_kernel,
        out_shape=[
            jax.ShapeDtypeStruct((surf, columns), F32),
            jax.ShapeDtypeStruct((surf, cells), F32),
            jax.ShapeDtypeStruct((levels, cells), F32),
        ],
        in_specs=[hbm] * 2 + [vmem] * 4,
        out_specs=[vmem, hbm, hbm],
        scratch_shapes=[
            pltpu.SMEM(src_block.shape[1:], jnp.int32),
            pltpu.SMEM(src_block.shape[1:], jnp.int32),
            pltpu.VMEM((near, tiles * surf, 128), F32),
            pltpu.VMEM((near * (cells // width + 1), 8, 128), F32),
            pltpu.VMEM((near * (cells // width + 1), 8, 128), F32),
            pltpu.VMEM((columns // width, 8, width), F32),
            dma((4,)),
        ],
        compiler_params=pltpu.CompilerParams(vmem_limit_bytes=32 * 2**20),
        name="back",
    )(src_block, dst_block, fluxes, margin_weights, ocean_surface, ocean_levels)
    return ocean_surface, ocean_levels, atm_flux


def solution(mesh):
    return jax.shard_map(
        functools.partial(shards, mesh.shape["grp"], mesh.shape["dom"], mesh.shape["lev"]),
        mesh=mesh,
        in_specs=(
            P("lev", ("grp", "dom")),
            P("lev", ("grp", "dom")),
            P(("grp", "dom"), None, None, None),
            P(("grp", "dom"), None, None),
            P(("grp", "dom"), None, None),
            P(("grp", "dom")),
            P("lev", ("grp", "dom")),
            P("lev", ("grp", "dom")),
            P(("grp", "dom")),
            P("lev"),
            P(("grp", "dom"), None),
        ),
        out_specs=(P("lev", ("grp", "dom")), P("lev", ("grp", "dom")), P("lev", ("grp", "dom"))),
        check_vma=False,
    )
```

```python
import functools

import jax
import jax.numpy as jnp
from jax import lax
from jax.experimental import pallas as pl
from jax.experimental.pallas import tpu as pltpu
from jax.sharding import PartitionSpec as P

HW = 128
KAPPA = 0.5
ROWS = 24
MESH = pl.DeviceIdType.MESH
F32 = jnp.float32
BF16 = jnp.bfloat16


def dot(a, b):
    return jnp.dot(a, b, preferred_element_type=F32)


def forward_kernel(src_hbm, dst_hbm, surf_hbm, lev_hbm, w_hbm, out_ref, src, dst, surf_ref, lev_ref, w_ref, joint, blocks, even, odd, small, big):
    levels, surf = lev_ref.shape[0], surf_ref.shape[0]
    near, width, across = w_ref.shape
    slots = across // width
    count = even.shape[0] - 1
    arriving = [
        pltpu.make_async_copy(here, there, small.at[n])
        for n, (here, there) in enumerate([(lev_hbm, lev_ref), (surf_hbm, surf_ref), (src_hbm.at[0], src), (dst_hbm.at[0], dst)])
    ]
    weights = [pltpu.make_async_copy(w_hbm.at[0, o], w_ref.at[o], big.at[o]) for o in range(near)]
    for one in arriving + weights:
        one.start()
    joint[levels + surf :, :] = jnp.zeros_like(joint[levels + surf :, :])
    arriving[0].wait()
    arriving[1].wait()
    joint[0:levels, :] = lev_ref[...].astype(F32)
    joint[levels : levels + surf, :] = surf_ref[...].astype(F32)
    for pair in range(blocks.shape[0] // 2):
        both = joint[:, pair * 128 : pair * 128 + 128].astype(BF16)
        blocks[2 * pair] = both[:, :64]
        blocks[2 * pair + 1] = both[:, 64:]
    arriving[2].wait()
    arriving[3].wait()
    low = lax.broadcasted_iota(jnp.int32, (ROWS, 128), 1) < 64

    def offset(o, carry):
        pltpu.make_async_copy(w_hbm.at[0, o], w_ref.at[o], big.at[o]).wait()
        even[...] = jnp.zeros_like(even)
        odd[...] = jnp.zeros_like(odd)
        for pair in range(slots // 2):
            a, b = 2 * pair, 2 * pair + 1
            lhs = jnp.concatenate([blocks[src[o, a]], blocks[src[o, b]]], axis=0)
            got = dot(lhs, w_ref[o, :, pair * 128 : pair * 128 + 128]).astype(BF16).astype(F32)
            to_a, to_b = dst[o, a], dst[o, b]
            to_a = jnp.where(to_a < 0, count, to_a)
            to_b = jnp.where(to_b < 0, count, to_b)
            even[to_a] = even[to_a] + got[:ROWS]
            odd[to_b] = odd[to_b] + got[32 : 32 + ROWS]

        def joined(t):
            left = even[2 * t] + pltpu.roll(odd[2 * t], 64, 1)
            right = pltpu.roll(even[2 * t + 1], 64, 1) + odd[2 * t + 1]
            return jnp.where(low, left, right)

        for t in range(0, count // 2, 2):
            both = jnp.concatenate([joined(t), joined(t + 1)], axis=0)
            out_ref[o, t * ROWS : (t + 2) * ROWS, :] = both.astype(BF16)
        return carry

    lax.fori_loop(0, near, offset, 0)


def middle_kernel(
    grp_n, dom_n, lev_n,
    agg, ice_cover, ice_flux, ocean_state, drag, level_weights, neighbours,
    surf_out, lev_out, flux_out,
    sib, comb, recv, own, parts_of, tile_of, place_of, counts, around, ice8, state8, lw_rows, flat, flux_send, flux_recv, col_send, col_recv, edge_recv,
    sib_s, sib_r, far_s, far_r, halo_s, halo_r, col_s, col_r, edge_s, edge_r, flux_s, flux_r,
):
    grp, dom, lev = lax.axis_index("grp"), lax.axis_index("dom"), lax.axis_index("lev")
    parts = grp_n * dom_n
    p = grp * dom_n + dom
    core = lax.rem(dom, 2)
    levels, surf = lev_out.shape[0], surf_out.shape[0]
    cells = lev_out.shape[1]
    tiles = cells // 128
    near = agg.shape[0]

    def part(by):
        q = lax.rem(p + by + parts, parts)
        return (q // dom_n, lax.rem(q, dom_n), lev)

    def ring(by, over=0):
        return (grp, lax.rem(dom + by + dom_n, dom_n), lax.rem(lev + over, lev_n))

    sibling = (grp, dom + 1 - 2 * core, lev)

    barrier = pltpu.get_barrier_semaphore()
    greeted = 0
    for by in range(1, near):
        for sign in (1, -1):
            pl.semaphore_signal(barrier, inc=1, device_id=part(sign * by), device_id_type=MESH)
            greeted += 1
    for by in (1, -1):
        pl.semaphore_signal(barrier, inc=1, device_id=ring(by), device_id_type=MESH)
        greeted += 1
    for over in range(1, lev_n):
        for by in (0, 1, -1):
            pl.semaphore_signal(barrier, inc=1, device_id=ring(by, over), device_id_type=MESH)
            greeted += 1
    first = levels - 16
    ice8[...] = jnp.zeros_like(ice8)
    state8[...] = jnp.zeros_like(state8)
    ice8[first : first + surf, :] = ice_flux[...].astype(F32)
    state8[first : first + surf, :] = ocean_state[...].astype(F32)
    lw_rows[...] = jnp.zeros_like(lw_rows)
    for k in range(levels):
        lw_rows[k : k + 1, :] = jnp.full((1, 128), level_weights[k], F32)
    nb = neighbours.shape[0]
    place = neighbours[...] - HW
    place = jnp.where(place < 0, place + cells + 2 * HW, place)
    tile_of[...] = place >> 7
    place_of[...] = place & 127
    pl.semaphore_wait(barrier, greeted)

    def copy(src, dst, send, got, device):
        return pltpu.make_async_remote_copy(
            src_ref=src, dst_ref=dst, send_sem=send, recv_sem=got, device_id=device, device_id_type=MESH
        )

    sib_copies = [copy(agg.at[2 * m + 1], sib.at[m], sib_s.at[m], sib_r.at[m], sibling) for m in range(3)]
    sib_copies.append(copy(agg.at[7], sib.at[3], sib_s.at[3], sib_r.at[3], part(1)))
    far1 = copy(comb.at[0], recv.at[0], far_s.at[0], far_r.at[0], part(2))
    far2 = copy(comb.at[1], recv.at[1], far_s.at[1], far_r.at[1], part(4))
    far3 = copy(comb.at[2], recv.at[2], far_s.at[2], far_r.at[2], part(2))
    for m in reversed(range(4)):
        sib_copies[m].start()

    def wide(ref, n):
        return ref[n].astype(F32)

    sib_copies[3].wait_recv()
    sib_copies[2].wait_recv()
    comb[2] = (wide(agg, 6) + wide(sib, 3) + jnp.where(core == 0, wide(sib, 2), 0.0)).astype(BF16)
    far3.start()
    sib_copies[1].wait_recv()
    sib_copies[0].wait_recv()
    comb[0] = (wide(agg, 2) + wide(sib, core)).astype(BF16)
    far1.start()

    def count_cells(n, carry):
        lanes = pl.ds(pl.multiple_of(n * 128, 128), 128)
        row = lax.broadcasted_iota(jnp.int32, (128, 128), 0)
        spots, tile_rows = [], []
        for e in range(nb):
            spot = jnp.where(jnp.broadcast_to(place_of[e : e + 1, lanes], (128, 128)) == row, 1.0, 0.0)
            spots.append(spot.astype(BF16))
            tile_rows.append(jnp.broadcast_to(tile_of[e : e + 1, lanes], (16, 128)).astype(F32).astype(BF16))
        for h in range(counts.shape[0] // 128):
            total = None
            for e in range(nb):
                hit = tile_rows[e] == jnp.full((16, 128), h, BF16)
                term = jnp.where(jnp.concatenate([hit] * 8, axis=0), spots[e], jnp.zeros_like(spots[e]))
                total = term if total is None else total + term
            counts[h * 128 : h * 128 + 128, lanes] = total
        return carry

    early = 3 * tiles // 8
    lax.fori_loop(0, early, count_cells, 0)
    far3.wait_recv()
    comb[1] = (wide(agg, 4) + wide(sib, 1 + core) + wide(recv, 2)).astype(BF16)
    far2.start()
    lax.fori_loop(early, tiles, count_cells, 0)

    far1.wait_recv()
    far2.wait_recv()

    is_surf = lax.broadcasted_iota(jnp.int32, (8, 128), 0) >= first
    for t in range(0, tiles, 2):
        rows = slice(t * ROWS, (t + 2) * ROWS)
        total = agg[0, rows, :].astype(F32) + recv[0, rows, :].astype(F32) + recv[1, rows, :].astype(F32)
        total = total + jnp.where(core == 1, sib[0, rows, :].astype(F32), 0.0)
        for u in range(2):
            lanes = slice((t + u) * 128, (t + u + 1) * 128)
            one = total[u * ROWS : (u + 1) * ROWS]
            share = ice_cover[:, lanes]
            tail = jnp.where(is_surf, (1.0 - share) * one[16:] + share * ice8[:, lanes], one[16:])
            merged = jnp.concatenate([one[:16], tail, jnp.zeros((8, 128), F32)], axis=0).astype(BF16)
            own[:, lanes] = merged
            col_send[:, lanes] = jnp.sum(lw_rows[...] * merged.astype(F32)[:ROWS], axis=0, keepdims=True)

    first_cells, last_cells = slice(0, HW), slice(cells - HW, cells)
    border = [
        copy(own.at[:, first_cells], own.at[:, cells : cells + HW], halo_s.at[0], halo_r.at[0], ring(-1)),
        copy(own.at[:, last_cells], own.at[:, cells + HW : cells + 2 * HW], halo_s.at[1], halo_r.at[1], ring(1)),
    ]
    for over in range(1, lev_n):
        border.append(copy(col_send, col_recv.at[over - 1], col_s.at[over - 1], col_r.at[over - 1], ring(0, over)))
    for over in range(lev_n):
        to, up = over, lev_n + over
        border.append(copy(col_send.at[:, first_cells], edge_recv.at[to], edge_s.at[to], edge_r.at[to], ring(-1, over)))
        border.append(copy(col_send.at[:, last_cells], edge_recv.at[up], edge_s.at[up], edge_r.at[up], ring(1, over)))
    for one in border:
        one.start()
    for one in border:
        one.wait_recv()
    inner, after, before = col_send[...], edge_recv[0], edge_recv[lev_n]
    for over in range(1, lev_n):
        inner = inner + col_recv[over - 1]
        after = after + edge_recv[over]
        before = before + edge_recv[lev_n + over]
    inner = jnp.concatenate([inner, after, before], axis=1)
    high = inner.astype(BF16).astype(F32)
    middle = (inner - high).astype(BF16).astype(F32)
    row = lax.broadcasted_iota(jnp.int32, (16, cells + 2 * HW), 0)
    split = jnp.where(row == 0, high, jnp.where(row == 1, middle, jnp.where(row == 2, inner - high - middle, 0.0)))
    parts_of[...] = split.astype(BF16)
    for c in range(cells // 256):
        lanes = slice(c * 256, c * 256 + 256)
        total = dot(jnp.concatenate([own[...], parts_of[...]], axis=0), counts[:, lanes])
        forcing = (1.0 - KAPPA) * own[:, lanes].astype(F32) + (KAPPA / nb) * total[:32]
        around[:, lanes] = forcing
        column = (1.0 - KAPPA) * inner[:, lanes] + (KAPPA / nb) * (total[32:33] + total[33:34] + total[34:35])
        flux = drag[:, lanes] * (state8[:, lanes] - forcing[16:ROWS] + column)
        for u in range(2):
            t = 2 * c + u
            flat[t * surf : (t + 1) * surf, :] = flux[first : first + surf, u * 128 : u * 128 + 128]
    flux_send[...] = flat[...].astype(BF16)
    flux_copies = [copy(flux_send, flux_recv.at[o - 1], flux_s.at[o - 1], flux_r.at[o - 1], part(-o)) for o in range(1, near)]
    for one in reversed(flux_copies):
        one.start()
    lev_out[...] = around[:levels, :]
    surf_out[...] = around[levels : levels + surf, :]
    flux_out[0] = flux_send[...]
    for o in range(1, near):
        flux_copies[o - 1].wait_recv()
        flux_out[o] = flux_recv[o - 1]

    for one in sib_copies + [far1, far2, far3] + border + flux_copies:
        one.wait_send()


def back_kernel(src_hbm, dst_hbm, flux_ref, w_ref, surf_ref, lev_ref, out_ref, surf_out, lev_out, src, dst, flat, even, odd, total, sems):
    surf = out_ref.shape[0]
    near, width, across = w_ref.shape[1:]
    slots = across // width
    count = even.shape[0] // near - 1
    copies = [
        pltpu.make_async_copy(here, there, sems.at[n])
        for n, (here, there) in enumerate([(src_hbm.at[0], src), (dst_hbm.at[0], dst), (surf_ref, surf_out), (lev_ref, lev_out)])
    ]
    for one in copies:
        one.start()
    total[...] = jnp.zeros_like(total)
    even[...] = jnp.zeros_like(even)
    odd[...] = jnp.zeros_like(odd)
    low = lax.broadcasted_iota(jnp.int32, (surf, 128), 1) < 64
    zero = jnp.zeros((surf, 128), F32)
    flat[...] = flux_ref[...].astype(F32)

    def spread(o, carry):
        base = o * (count + 1)
        for t in range(count // 2):
            here = flat[o, t * surf : (t + 1) * surf, :]
            there = pltpu.roll(here, 64, 1)
            even[base + 2 * t, 0:surf, :] = jnp.where(low, here, zero)
            odd[base + 2 * t, 0:surf, :] = jnp.where(low, zero, there)
            even[base + 2 * t + 1, 0:surf, :] = jnp.where(low, there, zero)
            odd[base + 2 * t + 1, 0:surf, :] = jnp.where(low, zero, here)
        return carry

    lax.fori_loop(0, near, spread, 0)
    copies[0].wait()
    copies[1].wait()

    def offset(o, carry):
        base = o * (count + 1)
        for pair in range(slots // 2):
            a, b = 2 * pair, 2 * pair + 1
            to_a, to_b = dst[o, a], dst[o, b]
            to_a = jnp.where(to_a < 0, count, to_a)
            to_b = jnp.where(to_b < 0, count, to_b)
            lhs = jnp.concatenate([even[base + to_a], odd[base + to_b]], axis=0).astype(BF16)
            got = lax.dot_general(
                lhs, w_ref[0, o, :, pair * 128 : pair * 128 + 128], (((1,), (1,)), ((), ())), preferred_element_type=F32
            )
            from_a, from_b = src[o, a], src[o, b]
            total[from_a] = total[from_a] + got[:8]
            total[from_b] = total[from_b] + got[8:]
        return carry

    lax.fori_loop(0, near, offset, 0)
    for pair in range(total.shape[0] // 2):
        both = jnp.concatenate([total[2 * pair], total[2 * pair + 1]], axis=1)
        out_ref[:, pair * 128 : pair * 128 + 128] = both[:surf]
    copies[2].wait()
    copies[3].wait()


def shards(
    grp_n, dom_n, lev_n,
    atm_surface, atm_levels, margin_weights, src_block, dst_block, ice_cover, ice_flux, ocean_state, drag, level_weights,
    neighbours,
):
    surf, columns = atm_surface.shape
    levels = atm_levels.shape[0]
    near, width, across = margin_weights.shape[1:]
    cells = ice_cover.shape[0]
    tiles = cells // 128
    flat_rows = tiles * ROWS
    hbm = pl.BlockSpec(memory_space=pltpu.HBM)
    dma = pltpu.SemaphoreType.DMA
    agg = pl.pallas_call(
        forward_kernel,
        out_shape=jax.ShapeDtypeStruct((near, flat_rows, 128), BF16),
        in_specs=[hbm] * 5,
        out_specs=pl.BlockSpec(memory_space=pltpu.VMEM),
        scratch_shapes=[
            pltpu.SMEM(src_block.shape[1:], jnp.int32),
            pltpu.SMEM(src_block.shape[1:], jnp.int32),
            pltpu.VMEM((surf, columns), BF16),
            pltpu.VMEM((levels, columns), BF16),
            pltpu.VMEM((near, width, across), BF16),
            pltpu.VMEM((32, columns), F32),
            pltpu.VMEM((columns // width, 32, width), BF16),
            pltpu.VMEM((cells // width + 1, ROWS, 128), F32),
            pltpu.VMEM((cells // width + 1, ROWS, 128), F32),
            dma((4,)),
            dma((near,)),
        ],
        compiler_params=pltpu.CompilerParams(vmem_limit_bytes=32 * 2**20),
        name="pieces",
    )(*[pltpu.with_memory_space_constraint(x, pltpu.HBM) for x in (src_block, dst_block, atm_surface, atm_levels, margin_weights)])

    vmem = pl.BlockSpec(memory_space=pltpu.VMEM)
    ocean_surface, ocean_levels, fluxes = pl.pallas_call(
        functools.partial(middle_kernel, grp_n, dom_n, lev_n),
        out_shape=[
            jax.ShapeDtypeStruct((surf, cells), F32),
            jax.ShapeDtypeStruct((levels, cells), F32),
            jax.ShapeDtypeStruct((near, tiles * surf, 128), BF16),
        ],
        in_specs=[vmem] * 5 + [pl.BlockSpec(memory_space=pltpu.SMEM), vmem],
        out_specs=[vmem] * 3,
        scratch_shapes=[
            pltpu.VMEM((4, flat_rows, 128), BF16),
            pltpu.VMEM((3, flat_rows, 128), BF16),
            pltpu.VMEM((3, flat_rows, 128), BF16),
            pltpu.VMEM((32, cells + 2 * HW), BF16),
            pltpu.VMEM((16, cells + 2 * HW), BF16),
            pltpu.VMEM((neighbours.shape[1], cells), jnp.int32),
            pltpu.VMEM((neighbours.shape[1], cells), jnp.int32),
            pltpu.VMEM((cells + 2 * HW, cells), BF16),
            pltpu.VMEM((32, cells), F32),
            pltpu.VMEM((8, cells), F32),
            pltpu.VMEM((8, cells), F32),
            pltpu.VMEM((ROWS, 128), F32),
            pltpu.VMEM((tiles * surf, 128), F32),
            pltpu.VMEM((tiles * surf, 128), BF16),
            pltpu.VMEM((near - 1, tiles * surf, 128), BF16),
            pltpu.VMEM((1, cells), F32),
            pltpu.VMEM((max(lev_n - 1, 1), 1, cells), F32),
            pltpu.VMEM((2 * lev_n, 1, HW), F32),
            dma((4,)), dma((4,)),
            dma((3,)), dma((3,)),
            dma((2,)), dma((2,)),
            dma((max(lev_n - 1, 1),)), dma((max(lev_n - 1, 1),)),
            dma((2 * lev_n,)), dma((2 * lev_n,)),
            dma((near - 1,)), dma((near - 1,)),
        ],
        compiler_params=pltpu.CompilerParams(collective_id=0, has_side_effects=True, vmem_limit_bytes=48 * 2**20),
        name="middle",
    )(agg, ice_cover.reshape(1, cells), ice_flux, ocean_state, drag.reshape(1, cells), level_weights, neighbours.T)

    atm_flux, ocean_surface, ocean_levels = pl.pallas_call(
        back_kernel,
        out_shape=[
            jax.ShapeDtypeStruct((surf, columns), F32),
            jax.ShapeDtypeStruct((surf, cells), F32),
            jax.ShapeDtypeStruct((levels, cells), F32),
        ],
        in_specs=[hbm] * 2 + [vmem] * 4,
        out_specs=[vmem, hbm, hbm],
        scratch_shapes=[
            pltpu.SMEM(src_block.shape[1:], jnp.int32),
            pltpu.SMEM(src_block.shape[1:], jnp.int32),
            pltpu.VMEM((near, tiles * surf, 128), F32),
            pltpu.VMEM((near * (cells // width + 1), 8, 128), F32),
            pltpu.VMEM((near * (cells // width + 1), 8, 128), F32),
            pltpu.VMEM((columns // width, 8, width), F32),
            dma((4,)),
        ],
        compiler_params=pltpu.CompilerParams(vmem_limit_bytes=32 * 2**20),
        name="back",
    )(src_block, dst_block, fluxes, margin_weights, ocean_surface, ocean_levels)
    return ocean_surface, ocean_levels, atm_flux


def solution(mesh):
    return jax.shard_map(
        functools.partial(shards, mesh.shape["grp"], mesh.shape["dom"], mesh.shape["lev"]),
        mesh=mesh,
        in_specs=(
            P("lev", ("grp", "dom")),
            P("lev", ("grp", "dom")),
            P(("grp", "dom"), None, None, None),
            P(("grp", "dom"), None, None),
            P(("grp", "dom"), None, None),
            P(("grp", "dom")),
            P("lev", ("grp", "dom")),
            P("lev", ("grp", "dom")),
            P(("grp", "dom")),
            P("lev"),
            P(("grp", "dom"), None),
        ),
        out_specs=(P("lev", ("grp", "dom")), P("lev", ("grp", "dom")), P("lev", ("grp", "dom"))),
        check_vma=False,
    )
```

```python
import functools

import jax
import jax.numpy as jnp
from jax import lax
from jax.experimental import pallas as pl
from jax.experimental.pallas import tpu as pltpu
from jax.sharding import PartitionSpec as P

HW = 128
KAPPA = 0.5
ROWS = 24
MESH = pl.DeviceIdType.MESH
F32 = jnp.float32
BF16 = jnp.bfloat16


def dot(a, b):
    return jnp.dot(a, b, preferred_element_type=F32)


def forward_kernel(src_hbm, dst_hbm, surf_hbm, lev_hbm, w_hbm, out_ref, src, dst, surf_ref, lev_ref, w_ref, joint, blocks, even, odd, small, big):
    levels, surf = lev_ref.shape[0], surf_ref.shape[0]
    near, width, across = w_ref.shape
    slots = across // width
    count = even.shape[0] - 1
    arriving = [
        pltpu.make_async_copy(here, there, small.at[n])
        for n, (here, there) in enumerate([(lev_hbm, lev_ref), (surf_hbm, surf_ref), (src_hbm.at[0], src), (dst_hbm.at[0], dst)])
    ]
    weights = [pltpu.make_async_copy(w_hbm.at[0, o], w_ref.at[o], big.at[o]) for o in range(near)]
    for one in arriving + weights:
        one.start()
    joint[levels + surf :, :] = jnp.zeros_like(joint[levels + surf :, :])
    arriving[0].wait()
    arriving[1].wait()
    joint[0:levels, :] = lev_ref[...].astype(F32)
    joint[levels : levels + surf, :] = surf_ref[...].astype(F32)
    for pair in range(blocks.shape[0] // 2):
        both = joint[:, pair * 128 : pair * 128 + 128].astype(BF16)
        blocks[2 * pair] = both[:, :64]
        blocks[2 * pair + 1] = both[:, 64:]
    arriving[2].wait()
    arriving[3].wait()
    low = lax.broadcasted_iota(jnp.int32, (ROWS, 128), 1) < 64

    def offset(o, carry):
        pltpu.make_async_copy(w_hbm.at[0, o], w_ref.at[o], big.at[o]).wait()
        even[...] = jnp.zeros_like(even)
        odd[...] = jnp.zeros_like(odd)
        for pair in range(slots // 2):
            a, b = 2 * pair, 2 * pair + 1
            lhs = jnp.concatenate([blocks[src[o, a]], blocks[src[o, b]]], axis=0)
            got = dot(lhs, w_ref[o, :, pair * 128 : pair * 128 + 128]).astype(BF16).astype(F32)
            to_a, to_b = dst[o, a], dst[o, b]
            to_a = jnp.where(to_a < 0, count, to_a)
            to_b = jnp.where(to_b < 0, count, to_b)
            even[to_a] = even[to_a] + got[:ROWS]
            odd[to_b] = odd[to_b] + got[32 : 32 + ROWS]

        def joined(t):
            left = even[2 * t] + pltpu.roll(odd[2 * t], 64, 1)
            right = pltpu.roll(even[2 * t + 1], 64, 1) + odd[2 * t + 1]
            return jnp.where(low, left, right)

        for t in range(0, count // 2, 2):
            both = jnp.concatenate([joined(t), joined(t + 1)], axis=0)
            out_ref[o, t * ROWS : (t + 2) * ROWS, :] = both.astype(BF16)
        return carry

    lax.fori_loop(0, near, offset, 0)


def middle_kernel(
    grp_n, dom_n, lev_n,
    agg, ice_cover, ice_flux, ocean_state, drag, level_weights, neighbours,
    surf_out, lev_out, flux_out,
    sib, comb, recv, own, halo, tile_of, place_of, counts, around, ice8, state8, lw_rows, flat, flux_send, flux_recv, col_send, col_recv,
    sib_s, sib_r, far_s, far_r, halo_s, halo_r, col_s, col_r, flux_s, flux_r,
):
    grp, dom, lev = lax.axis_index("grp"), lax.axis_index("dom"), lax.axis_index("lev")
    parts = grp_n * dom_n
    p = grp * dom_n + dom
    core = lax.rem(dom, 2)
    levels, surf = lev_out.shape[0], surf_out.shape[0]
    cells = lev_out.shape[1]
    tiles = cells // 128
    near = agg.shape[0]

    def part(by):
        q = lax.rem(p + by + parts, parts)
        return (q // dom_n, lax.rem(q, dom_n), lev)

    def ring(by):
        return (grp, lax.rem(dom + by + dom_n, dom_n), lev)

    def column_peer(by):
        return (grp, dom, lax.rem(lev + by, lev_n))

    sibling = (grp, dom + 1 - 2 * core, lev)

    barrier = pltpu.get_barrier_semaphore()
    greeted = 0
    for by in range(1, near):
        for sign in (1, -1):
            pl.semaphore_signal(barrier, inc=1, device_id=part(sign * by), device_id_type=MESH)
            greeted += 1
    for by in (1, -1):
        pl.semaphore_signal(barrier, inc=1, device_id=ring(by), device_id_type=MESH)
        greeted += 1
    for by in range(1, lev_n):
        pl.semaphore_signal(barrier, inc=1, device_id=column_peer(by), device_id_type=MESH)
        greeted += 1
    pl.semaphore_wait(barrier, greeted)

    def copy(src, dst, send, got, device):
        return pltpu.make_async_remote_copy(
            src_ref=src, dst_ref=dst, send_sem=send, recv_sem=got, device_id=device, device_id_type=MESH
        )

    sib_copies = [copy(agg.at[2 * m + 1], sib.at[m], sib_s.at[m], sib_r.at[m], sibling) for m in range(3)]
    sib_copies.append(copy(agg.at[7], sib.at[3], sib_s.at[3], sib_r.at[3], part(1)))
    far1 = copy(comb.at[0], recv.at[0], far_s.at[0], far_r.at[0], part(2))
    far2 = copy(comb.at[1], recv.at[1], far_s.at[1], far_r.at[1], part(4))
    far3 = copy(comb.at[2], recv.at[2], far_s.at[2], far_r.at[2], part(2))
    for m in reversed(range(4)):
        sib_copies[m].start()

    def wide(ref, n):
        return ref[n].astype(F32)

    first = levels - 16
    ice8[...] = jnp.zeros_like(ice8)
    state8[...] = jnp.zeros_like(state8)
    ice8[first : first + surf, :] = ice_flux[...].astype(F32)
    state8[first : first + surf, :] = ocean_state[...].astype(F32)
    lw_rows[...] = jnp.zeros_like(lw_rows)
    for k in range(levels):
        lw_rows[k : k + 1, :] = jnp.full((1, 128), level_weights[k], F32)
    nb = neighbours.shape[0]
    place = neighbours[...] - HW
    place = jnp.where(place < 0, place + cells + 2 * HW, place)
    tile_of[...] = place >> 7
    place_of[...] = place & 127
    def count_cells(n, carry):
        lanes = pl.ds(pl.multiple_of(n * 128, 128), 128)
        row = lax.broadcasted_iota(jnp.int32, (128, 128), 0)
        spots, tile_rows = [], []
        for e in range(nb):
            spot = jnp.where(jnp.broadcast_to(place_of[e : e + 1, lanes], (128, 128)) == row, 1.0, 0.0)
            spots.append(spot.astype(BF16))
            tile_rows.append(jnp.broadcast_to(tile_of[e : e + 1, lanes], (16, 128)).astype(F32).astype(BF16))
        for h in range(counts.shape[0] // 128):
            total = None
            for e in range(nb):
                hit = tile_rows[e] == jnp.full((16, 128), h, BF16)
                term = jnp.where(jnp.concatenate([hit] * 8, axis=0), spots[e], jnp.zeros_like(spots[e]))
                total = term if total is None else total + term
            counts[h * 128 : h * 128 + 128, lanes] = total
        return carry

    lax.fori_loop(0, 5 * tiles // 16, count_cells, 0)
    sib_copies[3].wait_recv()
    sib_copies[2].wait_recv()
    comb[2] = (wide(agg, 6) + wide(sib, 3) + jnp.where(core == 0, wide(sib, 2), 0.0)).astype(BF16)
    far3.start()
    sib_copies[1].wait_recv()
    sib_copies[0].wait_recv()
    comb[0] = (wide(agg, 2) + wide(sib, core)).astype(BF16)
    far1.start()

    lax.fori_loop(5 * tiles // 16, 5 * tiles // 8, count_cells, 0)
    far3.wait_recv()
    comb[1] = (wide(agg, 4) + wide(sib, 1 + core) + wide(recv, 2)).astype(BF16)
    far2.start()
    lax.fori_loop(5 * tiles // 8, tiles, count_cells, 0)

    far1.wait_recv()
    far2.wait_recv()

    is_surf = lax.broadcasted_iota(jnp.int32, (8, 128), 0) >= first
    def merge(t):
        rows = slice(t * ROWS, (t + 2) * ROWS)
        total = agg[0, rows, :].astype(F32) + recv[0, rows, :].astype(F32) + recv[1, rows, :].astype(F32)
        total = total + jnp.where(core == 1, sib[0, rows, :].astype(F32), 0.0)
        for u in range(2):
            lanes = slice((t + u) * 128, (t + u + 1) * 128)
            one = total[u * ROWS : (u + 1) * ROWS]
            share = ice_cover[:, lanes]
            tail = jnp.where(is_surf, (1.0 - share) * one[16:] + share * ice8[:, lanes], one[16:])
            own[:, lanes] = jnp.concatenate([one[:16], tail, jnp.zeros((8, 128), F32)], axis=0).astype(BF16)

    merge(0)
    merge(tiles - 2)
    to_prev = copy(own.at[:, 0:HW], halo.at[:, 0:HW], halo_s.at[0], halo_r.at[0], ring(-1))
    to_next = copy(own.at[:, cells - HW : cells], halo.at[:, HW : 2 * HW], halo_s.at[1], halo_r.at[1], ring(1))
    to_prev.start()
    to_next.start()
    for t in range(2, tiles - 2, 2):
        merge(t)
    for c in range(cells // 256):
        lanes = slice(c * 256, c * 256 + 256)
        around[:, lanes] = dot(own[...], counts[0:cells, lanes])
    to_prev.wait_recv()
    to_next.wait_recv()
    weight = jnp.concatenate([lw_rows[...], lw_rows[...]], axis=1)
    for c in range(cells // 256):
        lanes = slice(c * 256, c * 256 + 256)
        total = around[:, lanes] + dot(halo[...], counts[cells : cells + 2 * HW, lanes])
        forcing = (1.0 - KAPPA) * own[:, lanes].astype(F32) + (KAPPA / nb) * total
        around[:, lanes] = forcing
        col_send[:, lanes] = jnp.sum(weight * forcing[:ROWS], axis=0, keepdims=True)

    col_copies = [copy(col_send, col_recv.at[by - 1], col_s.at[by - 1], col_r.at[by - 1], column_peer(by)) for by in range(1, lev_n)]
    for one in col_copies:
        one.start()
    lev_out[...] = around[:levels, :]
    surf_out[...] = around[levels : levels + surf, :]
    for one in col_copies:
        one.wait_recv()
    column = col_send[...]
    for by in range(1, lev_n):
        column = column + col_recv[by - 1]
    flux = drag[...] * (state8[...] - around[16:ROWS, :] + column)
    for t in range(tiles):
        flat[t * surf : (t + 1) * surf, :] = flux[first : first + surf, t * 128 : t * 128 + 128]
    flux_send[...] = flat[...].astype(BF16)
    flux_copies = [copy(flux_send, flux_recv.at[o - 1], flux_s.at[o - 1], flux_r.at[o - 1], part(-o)) for o in range(1, near)]
    for one in reversed(flux_copies):
        one.start()
    flux_out[0] = flux_send[...]
    for o in range(1, near):
        flux_copies[o - 1].wait_recv()
        flux_out[o] = flux_recv[o - 1]

    for one in sib_copies + [far1, far2, far3, to_prev, to_next] + col_copies + flux_copies:
        one.wait_send()


def back_kernel(src_hbm, dst_hbm, flux_ref, w_ref, surf_ref, lev_ref, out_ref, surf_out, lev_out, src, dst, flat, even, odd, total, sems):
    surf = out_ref.shape[0]
    near, width, across = w_ref.shape[1:]
    slots = across // width
    count = even.shape[0] // near - 1
    copies = [
        pltpu.make_async_copy(here, there, sems.at[n])
        for n, (here, there) in enumerate([(src_hbm.at[0], src), (dst_hbm.at[0], dst), (surf_ref, surf_out), (lev_ref, lev_out)])
    ]
    for one in copies:
        one.start()
    total[...] = jnp.zeros_like(total)
    low = lax.broadcasted_iota(jnp.int32, (surf, 128), 1) < 64
    zero = jnp.zeros((surf, 128), F32)
    flat[...] = flux_ref[...].astype(F32)

    def spread(o, carry):
        base = o * (count + 1)
        even[base + count] = jnp.zeros((8, 128), F32)
        odd[base + count] = jnp.zeros((8, 128), F32)
        for t in range(count // 2):
            here = flat[o, t * surf : (t + 1) * surf, :]
            there = pltpu.roll(here, 64, 1)
            even[base + 2 * t, 0:surf, :] = jnp.where(low, here, zero)
            odd[base + 2 * t, 0:surf, :] = jnp.where(low, zero, there)
            even[base + 2 * t + 1, 0:surf, :] = jnp.where(low, there, zero)
            odd[base + 2 * t + 1, 0:surf, :] = jnp.where(low, zero, here)
        return carry

    lax.fori_loop(0, near, spread, 0)
    copies[0].wait()
    copies[1].wait()

    def offset(o, carry):
        base = o * (count + 1)
        zero = jnp.zeros((16, 128), BF16)
        for quad in range(slots // 4):
            rows = []
            for half in range(2):
                to_a, to_b = dst[o, 4 * quad + 2 * half], dst[o, 4 * quad + 2 * half + 1]
                to_a = jnp.where(to_a < 0, count, to_a)
                to_b = jnp.where(to_b < 0, count, to_b)
                rows.append(jnp.concatenate([even[base + to_a], odd[base + to_b]], axis=0).astype(BF16))
            lhs = jnp.concatenate(
                [jnp.concatenate([rows[0], zero], axis=1), jnp.concatenate([zero, rows[1]], axis=1)], axis=0
            )
            got = lax.dot_general(
                lhs, w_ref[0, o, :, quad * 256 : quad * 256 + 256], (((1,), (1,)), ((), ())), preferred_element_type=F32
            )
            for u in range(4):
                to = src[o, 4 * quad + u]
                total[u, to] = total[u, to] + got[8 * u : 8 * u + 8]
        return carry

    lax.fori_loop(0, near, offset, 0)
    def summed(b):
        return (total[0, b] + total[1, b]) + (total[2, b] + total[3, b])

    for pair in range(total.shape[1] // 2):
        both = jnp.concatenate([summed(2 * pair), summed(2 * pair + 1)], axis=1)
        out_ref[:, pair * 128 : pair * 128 + 128] = both[:surf]
    copies[2].wait()
    copies[3].wait()


def shards(
    grp_n, dom_n, lev_n,
    atm_surface, atm_levels, margin_weights, src_block, dst_block, ice_cover, ice_flux, ocean_state, drag, level_weights,
    neighbours,
):
    surf, columns = atm_surface.shape
    levels = atm_levels.shape[0]
    near, width, across = margin_weights.shape[1:]
    cells = ice_cover.shape[0]
    tiles = cells // 128
    flat_rows = tiles * ROWS
    hbm = pl.BlockSpec(memory_space=pltpu.HBM)
    dma = pltpu.SemaphoreType.DMA
    agg = pl.pallas_call(
        forward_kernel,
        out_shape=jax.ShapeDtypeStruct((near, flat_rows, 128), BF16),
        in_specs=[hbm] * 5,
        out_specs=pl.BlockSpec(memory_space=pltpu.VMEM),
        scratch_shapes=[
            pltpu.SMEM(src_block.shape[1:], jnp.int32),
            pltpu.SMEM(src_block.shape[1:], jnp.int32),
            pltpu.VMEM((surf, columns), BF16),
            pltpu.VMEM((levels, columns), BF16),
            pltpu.VMEM((near, width, across), BF16),
            pltpu.VMEM((32, columns), F32),
            pltpu.VMEM((columns // width, 32, width), BF16),
            pltpu.VMEM((cells // width + 1, ROWS, 128), F32),
            pltpu.VMEM((cells // width + 1, ROWS, 128), F32),
            dma((4,)),
            dma((near,)),
        ],
        compiler_params=pltpu.CompilerParams(vmem_limit_bytes=32 * 2**20),
        name="pieces",
    )(*[pltpu.with_memory_space_constraint(x, pltpu.HBM) for x in (src_block, dst_block, atm_surface, atm_levels, margin_weights)])

    vmem = pl.BlockSpec(memory_space=pltpu.VMEM)
    ocean_surface, ocean_levels, fluxes = pl.pallas_call(
        functools.partial(middle_kernel, grp_n, dom_n, lev_n),
        out_shape=[
            jax.ShapeDtypeStruct((surf, cells), F32),
            jax.ShapeDtypeStruct((levels, cells), F32),
            jax.ShapeDtypeStruct((near, tiles * surf, 128), BF16),
        ],
        in_specs=[vmem] * 5 + [pl.BlockSpec(memory_space=pltpu.SMEM), vmem],
        out_specs=[vmem] * 3,
        scratch_shapes=[
            pltpu.VMEM((4, flat_rows, 128), BF16),
            pltpu.VMEM((3, flat_rows, 128), BF16),
            pltpu.VMEM((3, flat_rows, 128), BF16),
            pltpu.VMEM((32, cells), BF16),
            pltpu.VMEM((32, 2 * HW), BF16),
            pltpu.VMEM((neighbours.shape[1], cells), jnp.int32),
            pltpu.VMEM((neighbours.shape[1], cells), jnp.int32),
            pltpu.VMEM((cells + 2 * HW, cells), BF16),
            pltpu.VMEM((32, cells), F32),
            pltpu.VMEM((8, cells), F32),
            pltpu.VMEM((8, cells), F32),
            pltpu.VMEM((ROWS, 128), F32),
            pltpu.VMEM((tiles * surf, 128), F32),
            pltpu.VMEM((tiles * surf, 128), BF16),
            pltpu.VMEM((near - 1, tiles * surf, 128), BF16),
            pltpu.VMEM((1, cells), F32),
            pltpu.VMEM((max(lev_n - 1, 1), 1, cells), F32),
            dma((4,)), dma((4,)),
            dma((3,)), dma((3,)),
            dma((2,)), dma((2,)),
            dma((3,)), dma((3,)),
            dma((near - 1,)), dma((near - 1,)),
        ],
        compiler_params=pltpu.CompilerParams(collective_id=0, has_side_effects=True, vmem_limit_bytes=48 * 2**20),
        name="middle",
    )(agg, ice_cover.reshape(1, cells), ice_flux, ocean_state, drag.reshape(1, cells), level_weights, neighbours.T)

    atm_flux, ocean_surface, ocean_levels = pl.pallas_call(
        back_kernel,
        out_shape=[
            jax.ShapeDtypeStruct((surf, columns), F32),
            jax.ShapeDtypeStruct((surf, cells), F32),
            jax.ShapeDtypeStruct((levels, cells), F32),
        ],
        in_specs=[hbm] * 2 + [vmem] * 4,
        out_specs=[vmem, hbm, hbm],
        scratch_shapes=[
            pltpu.SMEM(src_block.shape[1:], jnp.int32),
            pltpu.SMEM(src_block.shape[1:], jnp.int32),
            pltpu.VMEM((near, tiles * surf, 128), F32),
            pltpu.VMEM((near * (cells // width + 1), 8, 128), F32),
            pltpu.VMEM((near * (cells // width + 1), 8, 128), F32),
            pltpu.VMEM((4, columns // width, 8, width), F32),
            dma((4,)),
        ],
        compiler_params=pltpu.CompilerParams(vmem_limit_bytes=32 * 2**20),
        name="back",
    )(src_block, dst_block, fluxes, margin_weights, ocean_surface, ocean_levels)
    return ocean_surface, ocean_levels, atm_flux


def solution(mesh):
    return jax.shard_map(
        functools.partial(shards, mesh.shape["grp"], mesh.shape["dom"], mesh.shape["lev"]),
        mesh=mesh,
        in_specs=(
            P("lev", ("grp", "dom")),
            P("lev", ("grp", "dom")),
            P(("grp", "dom"), None, None, None),
            P(("grp", "dom"), None, None),
            P(("grp", "dom"), None, None),
            P(("grp", "dom")),
            P("lev", ("grp", "dom")),
            P("lev", ("grp", "dom")),
            P(("grp", "dom")),
            P("lev"),
            P(("grp", "dom"), None),
        ),
        out_specs=(P("lev", ("grp", "dom")), P("lev", ("grp", "dom")), P("lev", ("grp", "dom"))),
        check_vma=False,
    )
```

```python
import functools

import jax
import jax.numpy as jnp
from jax import lax
from jax.experimental import pallas as pl
from jax.experimental.pallas import tpu as pltpu
from jax.sharding import PartitionSpec as P

HW = 128
KAPPA = 0.5
ROWS = 24
MESH = pl.DeviceIdType.MESH
F32 = jnp.float32
BF16 = jnp.bfloat16


def dot(a, b):
    return jnp.dot(a, b, preferred_element_type=F32)


def forward_kernel(src_hbm, dst_hbm, surf_hbm, lev_hbm, w_hbm, out_ref, src, dst, surf_ref, lev_ref, w_ref, joint, blocks, even, odd, small, big):
    levels, surf = lev_ref.shape[0], surf_ref.shape[0]
    near, width, across = w_ref.shape
    slots = across // width
    count = even.shape[0] - 1
    arriving = [
        pltpu.make_async_copy(here, there, small.at[n])
        for n, (here, there) in enumerate([(lev_hbm, lev_ref), (surf_hbm, surf_ref), (src_hbm.at[0], src), (dst_hbm.at[0], dst)])
    ]
    weights = [pltpu.make_async_copy(w_hbm.at[0, o], w_ref.at[o], big.at[o]) for o in range(near)]
    for one in arriving + weights:
        one.start()
    joint[levels + surf :, :] = jnp.zeros_like(joint[levels + surf :, :])
    arriving[0].wait()
    arriving[1].wait()
    joint[0:levels, :] = lev_ref[...].astype(F32)
    joint[levels : levels + surf, :] = surf_ref[...].astype(F32)
    for pair in range(blocks.shape[0] // 2):
        both = joint[:, pair * 128 : pair * 128 + 128].astype(BF16)
        blocks[2 * pair] = both[:, :64]
        blocks[2 * pair + 1] = both[:, 64:]
    arriving[2].wait()
    arriving[3].wait()
    low = lax.broadcasted_iota(jnp.int32, (ROWS, 128), 1) < 64

    def offset(o, carry):
        pltpu.make_async_copy(w_hbm.at[0, o], w_ref.at[o], big.at[o]).wait()
        even[...] = jnp.zeros_like(even)
        odd[...] = jnp.zeros_like(odd)
        for pair in range(slots // 2):
            a, b = 2 * pair, 2 * pair + 1
            lhs = jnp.concatenate([blocks[src[o, a]], blocks[src[o, b]]], axis=0)
            got = dot(lhs, w_ref[o, :, pair * 128 : pair * 128 + 128]).astype(BF16).astype(F32)
            to_a, to_b = dst[o, a], dst[o, b]
            to_a = jnp.where(to_a < 0, count, to_a)
            to_b = jnp.where(to_b < 0, count, to_b)
            even[to_a] = even[to_a] + got[:ROWS]
            odd[to_b] = odd[to_b] + got[32 : 32 + ROWS]

        def joined(t):
            left = even[2 * t] + pltpu.roll(odd[2 * t], 64, 1)
            right = pltpu.roll(even[2 * t + 1], 64, 1) + odd[2 * t + 1]
            return jnp.where(low, left, right)

        for t in range(0, count // 2, 2):
            both = jnp.concatenate([joined(t), joined(t + 1)], axis=0)
            out_ref[o, t * ROWS : (t + 2) * ROWS, :] = both.astype(BF16)
        return carry

    lax.fori_loop(0, near, offset, 0)


def middle_kernel(
    grp_n, dom_n, lev_n,
    agg, ice_cover, ice_flux, ocean_state, drag, level_weights, neighbours,
    surf_out, lev_out, flux_out,
    sib, comb, recv, own, halo, tile_of, place_of, counts, around, ice8, state8, lw_rows, flat, flux_send, flux_recv, col_send, col_recv,
    sib_s, sib_r, far_s, far_r, halo_s, halo_r, col_s, col_r, flux_s, flux_r,
):
    grp, dom, lev = lax.axis_index("grp"), lax.axis_index("dom"), lax.axis_index("lev")
    parts = grp_n * dom_n
    p = grp * dom_n + dom
    core = lax.rem(dom, 2)
    levels, surf = lev_out.shape[0], surf_out.shape[0]
    cells = lev_out.shape[1]
    tiles = cells // 128
    near = agg.shape[0]

    def part(by):
        q = lax.rem(p + by + parts, parts)
        return (q // dom_n, lax.rem(q, dom_n), lev)

    def ring(by):
        return (grp, lax.rem(dom + by + dom_n, dom_n), lev)

    def column_peer(by):
        return (grp, dom, lax.rem(lev + by, lev_n))

    sibling = (grp, dom + 1 - 2 * core, lev)

    barrier = pltpu.get_barrier_semaphore()
    greeted = 0
    for by in range(1, near):
        for sign in (1, -1):
            pl.semaphore_signal(barrier, inc=1, device_id=part(sign * by), device_id_type=MESH)
            greeted += 1
    for by in (1, -1):
        pl.semaphore_signal(barrier, inc=1, device_id=ring(by), device_id_type=MESH)
        greeted += 1
    for by in range(1, lev_n):
        pl.semaphore_signal(barrier, inc=1, device_id=column_peer(by), device_id_type=MESH)
        greeted += 1
    pl.semaphore_wait(barrier, greeted)

    def copy(src, dst, send, got, device):
        return pltpu.make_async_remote_copy(
            src_ref=src, dst_ref=dst, send_sem=send, recv_sem=got, device_id=device, device_id_type=MESH
        )

    half = agg.shape[1] // 2
    halves = [slice(0, half), slice(half, 2 * half)]
    to_core = [
        [copy(agg.at[2 * m + 1, h], sib.at[m, h], sib_s.at[m, n], sib_r.at[m, n], part(1) if m == 3 else sibling) for m in range(4)]
        for n, h in enumerate(halves)
    ]
    along = [
        [copy(comb.at[d, h], recv.at[d, h], far_s.at[d, n], far_r.at[d, n], part(2)) for d in range(3)]
        for n, h in enumerate(halves)
    ]
    for m in (3, 2, 1, 0):
        for n in range(2):
            to_core[n][m].start()

    def wide(ref, i, n):
        return ref[i, halves[n], :].astype(F32)

    first = levels - 16
    ice8[...] = jnp.zeros_like(ice8)
    state8[...] = jnp.zeros_like(state8)
    ice8[first : first + surf, :] = ice_flux[...].astype(F32)
    state8[first : first + surf, :] = ocean_state[...].astype(F32)
    lw_rows[...] = jnp.zeros_like(lw_rows)
    for k in range(levels):
        lw_rows[k : k + 1, :] = jnp.full((1, 128), level_weights[k], F32)
    nb = neighbours.shape[0]
    place = neighbours[...] - HW
    place = jnp.where(place < 0, place + cells + 2 * HW, place)
    tile_of[...] = place >> 7
    place_of[...] = place & 127
    def count_cells(n, carry):
        lanes = pl.ds(pl.multiple_of(n * 128, 128), 128)
        row = lax.broadcasted_iota(jnp.int32, (128, 128), 0)
        spots, tile_rows = [], []
        for e in range(nb):
            spot = jnp.where(jnp.broadcast_to(place_of[e : e + 1, lanes], (128, 128)) == row, 1.0, 0.0)
            spots.append(spot.astype(BF16))
            tile_rows.append(jnp.broadcast_to(tile_of[e : e + 1, lanes], (16, 128)).astype(F32).astype(BF16))
        for h in range(counts.shape[0] // 128):
            total = None
            for e in range(nb):
                hit = tile_rows[e] == jnp.full((16, 128), h, BF16)
                term = jnp.where(jnp.concatenate([hit] * 8, axis=0), spots[e], jnp.zeros_like(spots[e]))
                total = term if total is None else total + term
            counts[h * 128 : h * 128 + 128, lanes] = total
        return carry

    lax.fori_loop(0, tiles // 4, count_cells, 0)
    for n in range(2):
        to_core[n][3].wait_recv()
        to_core[n][2].wait_recv()
        far = wide(agg, 6, n) + wide(sib, 3, n) + jnp.where(core == 0, wide(sib, 2, n), 0.0)
        comb[2, halves[n], :] = far.astype(BF16)
        along[n][2].start()
    lax.fori_loop(tiles // 4, tiles // 2, count_cells, 0)
    for n in range(2):
        to_core[n][1].wait_recv()
        to_core[n][0].wait_recv()
    for n in range(2):
        along[n][2].wait_recv()
        comb[1, halves[n], :] = (wide(agg, 4, n) + wide(sib, 1 + core, n) + wide(recv, 2, n)).astype(BF16)
        along[n][1].start()
    lax.fori_loop(tiles // 2, 3 * tiles // 4, count_cells, 0)
    for n in range(2):
        along[n][1].wait_recv()
        comb[0, halves[n], :] = (wide(agg, 2, n) + wide(sib, core, n) + wide(recv, 1, n)).astype(BF16)
        along[n][0].start()
    lax.fori_loop(3 * tiles // 4, tiles, count_cells, 0)
    for n in range(2):
        along[n][0].wait_recv()

    is_surf = lax.broadcasted_iota(jnp.int32, (8, 128), 0) >= first
    def merge(t):
        rows = slice(t * ROWS, (t + 2) * ROWS)
        total = agg[0, rows, :].astype(F32) + recv[0, rows, :].astype(F32)
        total = total + jnp.where(core == 1, sib[0, rows, :].astype(F32), 0.0)
        for u in range(2):
            lanes = slice((t + u) * 128, (t + u + 1) * 128)
            one = total[u * ROWS : (u + 1) * ROWS]
            share = ice_cover[:, lanes]
            tail = jnp.where(is_surf, (1.0 - share) * one[16:] + share * ice8[:, lanes], one[16:])
            own[:, lanes] = jnp.concatenate([one[:16], tail, jnp.zeros((8, 128), F32)], axis=0).astype(BF16)

    merge(0)
    merge(tiles - 2)
    to_prev = copy(own.at[:, 0:HW], halo.at[:, 0:HW], halo_s.at[0], halo_r.at[0], ring(-1))
    to_next = copy(own.at[:, cells - HW : cells], halo.at[:, HW : 2 * HW], halo_s.at[1], halo_r.at[1], ring(1))
    to_prev.start()
    to_next.start()
    for t in range(2, tiles - 2, 2):
        merge(t)
    for c in range(cells // 256):
        lanes = slice(c * 256, c * 256 + 256)
        around[:, lanes] = dot(own[...], counts[0:cells, lanes])
    to_prev.wait_recv()
    to_next.wait_recv()
    weight = jnp.concatenate([lw_rows[...], lw_rows[...]], axis=1)
    for c in range(cells // 256):
        lanes = slice(c * 256, c * 256 + 256)
        total = around[:, lanes] + dot(halo[...], counts[cells : cells + 2 * HW, lanes])
        forcing = (1.0 - KAPPA) * own[:, lanes].astype(F32) + (KAPPA / nb) * total
        around[:, lanes] = forcing
        col_send[:, lanes] = jnp.sum(weight * forcing[:ROWS], axis=0, keepdims=True)

    col_copies = [copy(col_send, col_recv.at[by - 1], col_s.at[by - 1], col_r.at[by - 1], column_peer(by)) for by in range(1, lev_n)]
    for one in col_copies:
        one.start()
    lev_out[...] = around[:levels, :]
    surf_out[...] = around[levels : levels + surf, :]
    for one in col_copies:
        one.wait_recv()
    column = col_send[...]
    for by in range(1, lev_n):
        column = column + col_recv[by - 1]
    flux = drag[...] * (state8[...] - around[16:ROWS, :] + column)
    for t in range(tiles):
        flat[t * surf : (t + 1) * surf, :] = flux[first : first + surf, t * 128 : t * 128 + 128]
    flux_send[...] = flat[...].astype(BF16)
    flux_copies = [copy(flux_send, flux_recv.at[o - 1], flux_s.at[o - 1], flux_r.at[o - 1], part(-o)) for o in range(1, near)]
    for one in reversed(flux_copies):
        one.start()
    flux_out[0] = flux_send[...]
    for o in range(1, near):
        flux_copies[o - 1].wait_recv()
        flux_out[o] = flux_recv[o - 1]

    for one in to_core[0] + to_core[1] + along[0] + along[1] + [to_prev, to_next] + col_copies + flux_copies:
        one.wait_send()


def back_kernel(src_hbm, dst_hbm, flux_ref, w_ref, surf_ref, lev_ref, out_ref, surf_out, lev_out, src, dst, flat, even, odd, total, sems):
    surf = out_ref.shape[0]
    near, width, across = w_ref.shape[1:]
    slots = across // width
    count = even.shape[0] // near - 1
    copies = [
        pltpu.make_async_copy(here, there, sems.at[n])
        for n, (here, there) in enumerate([(src_hbm.at[0], src), (dst_hbm.at[0], dst), (surf_ref, surf_out), (lev_ref, lev_out)])
    ]
    for one in copies:
        one.start()
    total[...] = jnp.zeros_like(total)
    low = lax.broadcasted_iota(jnp.int32, (surf, 128), 1) < 64
    zero = jnp.zeros((surf, 128), F32)
    flat[...] = flux_ref[...].astype(F32)

    def spread(o, carry):
        base = o * (count + 1)
        even[base + count] = jnp.zeros((8, 128), F32)
        odd[base + count] = jnp.zeros((8, 128), F32)
        for t in range(count // 2):
            here = flat[o, t * surf : (t + 1) * surf, :]
            there = pltpu.roll(here, 64, 1)
            even[base + 2 * t, 0:surf, :] = jnp.where(low, here, zero)
            odd[base + 2 * t, 0:surf, :] = jnp.where(low, zero, there)
            even[base + 2 * t + 1, 0:surf, :] = jnp.where(low, there, zero)
            odd[base + 2 * t + 1, 0:surf, :] = jnp.where(low, zero, here)
        return carry

    lax.fori_loop(0, near, spread, 0)
    copies[0].wait()
    copies[1].wait()

    def offset(o, carry):
        base = o * (count + 1)
        zero = jnp.zeros((16, 128), BF16)
        for quad in range(slots // 4):
            rows = []
            for half in range(2):
                to_a, to_b = dst[o, 4 * quad + 2 * half], dst[o, 4 * quad + 2 * half + 1]
                to_a = jnp.where(to_a < 0, count, to_a)
                to_b = jnp.where(to_b < 0, count, to_b)
                rows.append(jnp.concatenate([even[base + to_a], odd[base + to_b]], axis=0).astype(BF16))
            lhs = jnp.concatenate(
                [jnp.concatenate([rows[0], zero], axis=1), jnp.concatenate([zero, rows[1]], axis=1)], axis=0
            )
            got = lax.dot_general(
                lhs, w_ref[0, o, :, quad * 256 : quad * 256 + 256], (((1,), (1,)), ((), ())), preferred_element_type=F32
            )
            for u in range(4):
                to = src[o, 4 * quad + u]
                total[u, to] = total[u, to] + got[8 * u : 8 * u + 8]
        return carry

    lax.fori_loop(0, near, offset, 0)
    def summed(b):
        return (total[0, b] + total[1, b]) + (total[2, b] + total[3, b])

    for pair in range(total.shape[1] // 2):
        both = jnp.concatenate([summed(2 * pair), summed(2 * pair + 1)], axis=1)
        out_ref[:, pair * 128 : pair * 128 + 128] = both[:surf]
    copies[2].wait()
    copies[3].wait()


def shards(
    grp_n, dom_n, lev_n,
    atm_surface, atm_levels, margin_weights, src_block, dst_block, ice_cover, ice_flux, ocean_state, drag, level_weights,
    neighbours,
):
    surf, columns = atm_surface.shape
    levels = atm_levels.shape[0]
    near, width, across = margin_weights.shape[1:]
    cells = ice_cover.shape[0]
    tiles = cells // 128
    flat_rows = tiles * ROWS
    hbm = pl.BlockSpec(memory_space=pltpu.HBM)
    dma = pltpu.SemaphoreType.DMA
    agg = pl.pallas_call(
        forward_kernel,
        out_shape=jax.ShapeDtypeStruct((near, flat_rows, 128), BF16),
        in_specs=[hbm] * 5,
        out_specs=pl.BlockSpec(memory_space=pltpu.VMEM),
        scratch_shapes=[
            pltpu.SMEM(src_block.shape[1:], jnp.int32),
            pltpu.SMEM(src_block.shape[1:], jnp.int32),
            pltpu.VMEM((surf, columns), BF16),
            pltpu.VMEM((levels, columns), BF16),
            pltpu.VMEM((near, width, across), BF16),
            pltpu.VMEM((32, columns), F32),
            pltpu.VMEM((columns // width, 32, width), BF16),
            pltpu.VMEM((cells // width + 1, ROWS, 128), F32),
            pltpu.VMEM((cells // width + 1, ROWS, 128), F32),
            dma((4,)),
            dma((near,)),
        ],
        compiler_params=pltpu.CompilerParams(vmem_limit_bytes=32 * 2**20),
        name="pieces",
    )(*[pltpu.with_memory_space_constraint(x, pltpu.HBM) for x in (src_block, dst_block, atm_surface, atm_levels, margin_weights)])

    vmem = pl.BlockSpec(memory_space=pltpu.VMEM)
    ocean_surface, ocean_levels, fluxes = pl.pallas_call(
        functools.partial(middle_kernel, grp_n, dom_n, lev_n),
        out_shape=[
            jax.ShapeDtypeStruct((surf, cells), F32),
            jax.ShapeDtypeStruct((levels, cells), F32),
            jax.ShapeDtypeStruct((near, tiles * surf, 128), BF16),
        ],
        in_specs=[vmem] * 5 + [pl.BlockSpec(memory_space=pltpu.SMEM), vmem],
        out_specs=[vmem] * 3,
        scratch_shapes=[
            pltpu.VMEM((4, flat_rows, 128), BF16),
            pltpu.VMEM((3, flat_rows, 128), BF16),
            pltpu.VMEM((3, flat_rows, 128), BF16),
            pltpu.VMEM((32, cells), BF16),
            pltpu.VMEM((32, 2 * HW), BF16),
            pltpu.VMEM((neighbours.shape[1], cells), jnp.int32),
            pltpu.VMEM((neighbours.shape[1], cells), jnp.int32),
            pltpu.VMEM((cells + 2 * HW, cells), BF16),
            pltpu.VMEM((32, cells), F32),
            pltpu.VMEM((8, cells), F32),
            pltpu.VMEM((8, cells), F32),
            pltpu.VMEM((ROWS, 128), F32),
            pltpu.VMEM((tiles * surf, 128), F32),
            pltpu.VMEM((tiles * surf, 128), BF16),
            pltpu.VMEM((near - 1, tiles * surf, 128), BF16),
            pltpu.VMEM((1, cells), F32),
            pltpu.VMEM((max(lev_n - 1, 1), 1, cells), F32),
            dma((4, 2)), dma((4, 2)),
            dma((3, 2)), dma((3, 2)),
            dma((2,)), dma((2,)),
            dma((3,)), dma((3,)),
            dma((near - 1,)), dma((near - 1,)),
        ],
        compiler_params=pltpu.CompilerParams(collective_id=0, has_side_effects=True, vmem_limit_bytes=48 * 2**20),
        name="middle",
    )(agg, ice_cover.reshape(1, cells), ice_flux, ocean_state, drag.reshape(1, cells), level_weights, neighbours.T)

    atm_flux, ocean_surface, ocean_levels = pl.pallas_call(
        back_kernel,
        out_shape=[
            jax.ShapeDtypeStruct((surf, columns), F32),
            jax.ShapeDtypeStruct((surf, cells), F32),
            jax.ShapeDtypeStruct((levels, cells), F32),
        ],
        in_specs=[hbm] * 2 + [vmem] * 4,
        out_specs=[vmem, hbm, hbm],
        scratch_shapes=[
            pltpu.SMEM(src_block.shape[1:], jnp.int32),
            pltpu.SMEM(src_block.shape[1:], jnp.int32),
            pltpu.VMEM((near, tiles * surf, 128), F32),
            pltpu.VMEM((near * (cells // width + 1), 8, 128), F32),
            pltpu.VMEM((near * (cells // width + 1), 8, 128), F32),
            pltpu.VMEM((4, columns // width, 8, width), F32),
            dma((4,)),
        ],
        compiler_params=pltpu.CompilerParams(vmem_limit_bytes=32 * 2**20),
        name="back",
    )(src_block, dst_block, fluxes, margin_weights, ocean_surface, ocean_levels)
    return ocean_surface, ocean_levels, atm_flux


def solution(mesh):
    return jax.shard_map(
        functools.partial(shards, mesh.shape["grp"], mesh.shape["dom"], mesh.shape["lev"]),
        mesh=mesh,
        in_specs=(
            P("lev", ("grp", "dom")),
            P("lev", ("grp", "dom")),
            P(("grp", "dom"), None, None, None),
            P(("grp", "dom"), None, None),
            P(("grp", "dom"), None, None),
            P(("grp", "dom")),
            P("lev", ("grp", "dom")),
            P("lev", ("grp", "dom")),
            P(("grp", "dom")),
            P("lev"),
            P(("grp", "dom"), None),
        ),
        out_specs=(P("lev", ("grp", "dom")), P("lev", ("grp", "dom")), P("lev", ("grp", "dom"))),
        check_vma=False,
    )
```

```python
import functools

import jax
import jax.numpy as jnp
from jax import lax
from jax.experimental import pallas as pl
from jax.experimental.pallas import tpu as pltpu
from jax.sharding import PartitionSpec as P

HW = 128
KAPPA = 0.5
ROWS = 24
MESH = pl.DeviceIdType.MESH
F32 = jnp.float32
BF16 = jnp.bfloat16


def dot(a, b):
    return jnp.dot(a, b, preferred_element_type=F32)


def forward_kernel(src_hbm, dst_hbm, surf_hbm, lev_hbm, w_hbm, out_ref, src, dst, surf_ref, lev_ref, w_ref, joint, blocks, sums, small, big):
    levels, surf = lev_ref.shape[0], surf_ref.shape[0]
    near, width, across = w_ref.shape
    slots = across // width
    tiles = sums.shape[0] - 1
    arriving = [
        pltpu.make_async_copy(here, there, small.at[n])
        for n, (here, there) in enumerate([(lev_hbm, lev_ref), (surf_hbm, surf_ref), (src_hbm.at[0], src), (dst_hbm.at[0], dst)])
    ]
    weights = [pltpu.make_async_copy(w_hbm.at[0, o], w_ref.at[o], big.at[o]) for o in range(near)]
    for one in arriving + weights:
        one.start()
    joint[levels + surf :, :] = jnp.zeros_like(joint[levels + surf :, :])
    arriving[0].wait()
    arriving[1].wait()
    joint[0:levels, :] = lev_ref[...].astype(F32)
    joint[levels : levels + surf, :] = surf_ref[...].astype(F32)
    for pair in range(blocks.shape[0] // 2):
        both = joint[:, pair * 128 : pair * 128 + 128].astype(BF16)
        blocks[2 * pair] = both[:, :64]
        blocks[2 * pair + 1] = both[:, 64:]
    arriving[2].wait()
    arriving[3].wait()
    side = lax.broadcasted_iota(jnp.int32, (ROWS, 128), 1) >> 6

    def offset(o, carry):
        pltpu.make_async_copy(w_hbm.at[0, o], w_ref.at[o], big.at[o]).wait()
        sums[...] = jnp.zeros_like(sums)
        for pair in range(slots // 2):
            slot = 2 * pair
            lhs = jnp.concatenate([blocks[src[o, slot]], blocks[src[o, slot + 1]]], axis=0)
            got = dot(lhs, w_ref[o, :, pair * 128 : pair * 128 + 128])
            for u in range(2):
                to = dst[o, slot + u]
                tile = jnp.where(to < 0, tiles, to >> 1)
                to_side = to & 1
                one = got[32 * u : 32 * u + ROWS].astype(BF16).astype(F32)
                one = pltpu.roll(one, 64 * (to_side ^ u), 1)
                sums[tile] = sums[tile] + jnp.where(side == to_side, one, 0.0)
        for t in range(0, tiles, 2):
            both = jnp.concatenate([sums[t], sums[t + 1]], axis=0)
            out_ref[o, t * ROWS : (t + 2) * ROWS, :] = both.astype(BF16)
        return carry

    lax.fori_loop(0, near, offset, 0)


def middle_kernel(
    grp_n, dom_n, lev_n,
    agg, ice_cover, ice_flux, ocean_state, drag, level_weights, neighbours,
    surf_out, lev_out, flux_out,
    sib, comb, recv, own, halo, tile_of, place_of, counts, around, ice8, state8, lw_rows, flat, flux_send, flux_recv, col_send, col_recv,
    sib_s, sib_r, far_s, far_r, halo_s, halo_r, col_s, col_r, flux_s, flux_r,
):
    grp, dom, lev = lax.axis_index("grp"), lax.axis_index("dom"), lax.axis_index("lev")
    parts = grp_n * dom_n
    p = grp * dom_n + dom
    core = lax.rem(dom, 2)
    levels, surf = lev_out.shape[0], surf_out.shape[0]
    cells = lev_out.shape[1]
    tiles = cells // 128
    near = agg.shape[0]

    def part(by):
        q = lax.rem(p + by + parts, parts)
        return (q // dom_n, lax.rem(q, dom_n), lev)

    def ring(by):
        return (grp, lax.rem(dom + by + dom_n, dom_n), lev)

    def column_peer(by):
        return (grp, dom, lax.rem(lev + by, lev_n))

    sibling = (grp, dom + 1 - 2 * core, lev)

    barrier = pltpu.get_barrier_semaphore()
    greeted = 0
    for by in range(1, near):
        for sign in (1, -1):
            pl.semaphore_signal(barrier, inc=1, device_id=part(sign * by), device_id_type=MESH)
            greeted += 1
    for by in (1, -1):
        pl.semaphore_signal(barrier, inc=1, device_id=ring(by), device_id_type=MESH)
        greeted += 1
    for by in range(1, lev_n):
        pl.semaphore_signal(barrier, inc=1, device_id=column_peer(by), device_id_type=MESH)
        greeted += 1
    pl.semaphore_wait(barrier, greeted)

    def copy(src, dst, send, got, device):
        return pltpu.make_async_remote_copy(
            src_ref=src, dst_ref=dst, send_sem=send, recv_sem=got, device_id=device, device_id_type=MESH
        )

    sib_copies = [copy(agg.at[2 * m + 1], sib.at[m], sib_s.at[m], sib_r.at[m], sibling) for m in range(3)]
    sib_copies.append(copy(agg.at[7], sib.at[3], sib_s.at[3], sib_r.at[3], part(1)))
    far1 = copy(comb.at[0], recv.at[0], far_s.at[0], far_r.at[0], part(2))
    far2 = copy(comb.at[1], recv.at[1], far_s.at[1], far_r.at[1], part(4))
    far3 = copy(comb.at[2], recv.at[2], far_s.at[2], far_r.at[2], part(2))
    for m in reversed(range(4)):
        sib_copies[m].start()

    def wide(ref, n):
        return ref[n].astype(F32)

    first = levels - 16
    ice8[...] = jnp.zeros_like(ice8)
    state8[...] = jnp.zeros_like(state8)
    ice8[first : first + surf, :] = ice_flux[...].astype(F32)
    state8[first : first + surf, :] = ocean_state[...].astype(F32)
    lw_rows[...] = jnp.zeros_like(lw_rows)
    for k in range(levels):
        lw_rows[k : k + 1, :] = jnp.full((1, 128), level_weights[k], F32)
    nb = neighbours.shape[0]
    place = neighbours[...] - HW
    place = jnp.where(place < 0, place + cells + 2 * HW, place)
    tile_of[...] = place >> 7
    place_of[...] = place & 127
    def count_cells(n, carry):
        lanes = pl.ds(pl.multiple_of(n * 128, 128), 128)
        row = lax.broadcasted_iota(jnp.int32, (128, 128), 0)
        spots, tile_rows = [], []
        for e in range(nb):
            spot = jnp.where(jnp.broadcast_to(place_of[e : e + 1, lanes], (128, 128)) == row, 1.0, 0.0)
            spots.append(spot.astype(BF16))
            tile_rows.append(jnp.broadcast_to(tile_of[e : e + 1, lanes], (16, 128)).astype(F32).astype(BF16))
        for h in range(counts.shape[0] // 128):
            total = None
            for e in range(nb):
                hit = tile_rows[e] == jnp.full((16, 128), h, BF16)
                term = jnp.where(jnp.concatenate([hit] * 8, axis=0), spots[e], jnp.zeros_like(spots[e]))
                total = term if total is None else total + term
            counts[h * 128 : h * 128 + 128, lanes] = total
        return carry

    lax.fori_loop(0, 5 * tiles // 16, count_cells, 0)
    sib_copies[3].wait_recv()
    sib_copies[2].wait_recv()
    comb[2] = (wide(agg, 6) + wide(sib, 3) + jnp.where(core == 0, wide(sib, 2), 0.0)).astype(BF16)
    far3.start()
    sib_copies[1].wait_recv()
    sib_copies[0].wait_recv()
    comb[0] = (wide(agg, 2) + wide(sib, core)).astype(BF16)
    far1.start()

    lax.fori_loop(5 * tiles // 16, 5 * tiles // 8, count_cells, 0)
    far3.wait_recv()
    comb[1] = (wide(agg, 4) + wide(sib, 1 + core) + wide(recv, 2)).astype(BF16)
    far2.start()
    lax.fori_loop(5 * tiles // 8, tiles, count_cells, 0)

    far1.wait_recv()
    far2.wait_recv()

    is_surf = lax.broadcasted_iota(jnp.int32, (8, 128), 0) >= first
    def merge(t):
        rows = slice(t * ROWS, (t + 2) * ROWS)
        total = agg[0, rows, :].astype(F32) + recv[0, rows, :].astype(F32) + recv[1, rows, :].astype(F32)
        total = total + jnp.where(core == 1, sib[0, rows, :].astype(F32), 0.0)
        for u in range(2):
            lanes = slice((t + u) * 128, (t + u + 1) * 128)
            one = total[u * ROWS : (u + 1) * ROWS]
            share = ice_cover[:, lanes]
            tail = jnp.where(is_surf, (1.0 - share) * one[16:] + share * ice8[:, lanes], one[16:])
            own[:, lanes] = jnp.concatenate([one[:16], tail, jnp.zeros((8, 128), F32)], axis=0).astype(BF16)

    merge(0)
    merge(tiles - 2)
    to_prev = copy(own.at[:, 0:HW], halo.at[:, 0:HW], halo_s.at[0], halo_r.at[0], ring(-1))
    to_next = copy(own.at[:, cells - HW : cells], halo.at[:, HW : 2 * HW], halo_s.at[1], halo_r.at[1], ring(1))
    to_prev.start()
    to_next.start()
    for t in range(2, tiles - 2, 2):
        merge(t)
    for c in range(cells // 256):
        lanes = slice(c * 256, c * 256 + 256)
        around[:, lanes] = dot(own[...], counts[0:cells, lanes])
    to_prev.wait_recv()
    to_next.wait_recv()
    weight = jnp.concatenate([lw_rows[...], lw_rows[...]], axis=1)
    for c in range(cells // 256):
        lanes = slice(c * 256, c * 256 + 256)
        total = around[:, lanes] + dot(halo[...], counts[cells : cells + 2 * HW, lanes])
        forcing = (1.0 - KAPPA) * own[:, lanes].astype(F32) + (KAPPA / nb) * total
        around[:, lanes] = forcing
        col_send[:, lanes] = jnp.sum(weight * forcing[:ROWS], axis=0, keepdims=True)

    col_copies = [copy(col_send, col_recv.at[by - 1], col_s.at[by - 1], col_r.at[by - 1], column_peer(by)) for by in range(1, lev_n)]
    for one in col_copies:
        one.start()
    lev_out[...] = around[:levels, :]
    surf_out[...] = around[levels : levels + surf, :]
    for one in col_copies:
        one.wait_recv()
    column = col_send[...]
    for by in range(1, lev_n):
        column = column + col_recv[by - 1]
    flux = drag[...] * (state8[...] - around[16:ROWS, :] + column)
    for t in range(tiles):
        flat[t * surf : (t + 1) * surf, :] = flux[first : first + surf, t * 128 : t * 128 + 128]
    flux_send[...] = flat[...].astype(BF16)
    flux_copies = [copy(flux_send, flux_recv.at[o - 1], flux_s.at[o - 1], flux_r.at[o - 1], part(-o)) for o in range(1, near)]
    for one in reversed(flux_copies):
        one.start()
    flux_out[0] = flux_send[...]
    for o in range(1, near):
        flux_copies[o - 1].wait_recv()
        flux_out[o] = flux_recv[o - 1]

    for one in sib_copies + [far1, far2, far3, to_prev, to_next] + col_copies + flux_copies:
        one.wait_send()


def back_kernel(src_hbm, dst_hbm, flux_ref, w_ref, surf_ref, lev_ref, out_ref, surf_out, lev_out, src, dst, flat, even, odd, total, sems):
    surf = out_ref.shape[0]
    near, width, across = w_ref.shape[1:]
    slots = across // width
    count = even.shape[0] // near - 1
    copies = [
        pltpu.make_async_copy(here, there, sems.at[n])
        for n, (here, there) in enumerate([(src_hbm.at[0], src), (dst_hbm.at[0], dst), (surf_ref, surf_out), (lev_ref, lev_out)])
    ]
    for one in copies:
        one.start()
    total[...] = jnp.zeros_like(total)
    low = lax.broadcasted_iota(jnp.int32, (surf, 128), 1) < 64
    zero = jnp.zeros((surf, 128), F32)
    flat[...] = flux_ref[...].astype(F32)

    def spread(o, carry):
        base = o * (count + 1)
        even[base + count] = jnp.zeros((8, 128), F32)
        odd[base + count] = jnp.zeros((8, 128), F32)
        for t in range(count // 2):
            here = flat[o, t * surf : (t + 1) * surf, :]
            there = pltpu.roll(here, 64, 1)
            even[base + 2 * t, 0:surf, :] = jnp.where(low, here, zero)
            odd[base + 2 * t, 0:surf, :] = jnp.where(low, zero, there)
            even[base + 2 * t + 1, 0:surf, :] = jnp.where(low, there, zero)
            odd[base + 2 * t + 1, 0:surf, :] = jnp.where(low, zero, here)
        return carry

    lax.fori_loop(0, near, spread, 0)
    copies[0].wait()
    copies[1].wait()

    def offset(o, carry):
        base = o * (count + 1)
        zero = jnp.zeros((16, 128), BF16)
        for quad in range(slots // 4):
            rows = []
            for half in range(2):
                to_a, to_b = dst[o, 4 * quad + 2 * half], dst[o, 4 * quad + 2 * half + 1]
                to_a = jnp.where(to_a < 0, count, to_a)
                to_b = jnp.where(to_b < 0, count, to_b)
                rows.append(jnp.concatenate([even[base + to_a], odd[base + to_b]], axis=0).astype(BF16))
            lhs = jnp.concatenate(
                [jnp.concatenate([rows[0], zero], axis=1), jnp.concatenate([zero, rows[1]], axis=1)], axis=0
            )
            got = lax.dot_general(
                lhs, w_ref[0, o, :, quad * 256 : quad * 256 + 256], (((1,), (1,)), ((), ())), preferred_element_type=F32
            )
            for u in range(4):
                to = src[o, 4 * quad + u]
                total[u, to] = total[u, to] + got[8 * u : 8 * u + 8]
        return carry

    lax.fori_loop(0, near, offset, 0)
    def summed(b):
        return (total[0, b] + total[1, b]) + (total[2, b] + total[3, b])

    for pair in range(total.shape[1] // 2):
        both = jnp.concatenate([summed(2 * pair), summed(2 * pair + 1)], axis=1)
        out_ref[:, pair * 128 : pair * 128 + 128] = both[:surf]
    copies[2].wait()
    copies[3].wait()


def shards(
    grp_n, dom_n, lev_n,
    atm_surface, atm_levels, margin_weights, src_block, dst_block, ice_cover, ice_flux, ocean_state, drag, level_weights,
    neighbours,
):
    surf, columns = atm_surface.shape
    levels = atm_levels.shape[0]
    near, width, across = margin_weights.shape[1:]
    cells = ice_cover.shape[0]
    tiles = cells // 128
    flat_rows = tiles * ROWS
    hbm = pl.BlockSpec(memory_space=pltpu.HBM)
    dma = pltpu.SemaphoreType.DMA
    agg = pl.pallas_call(
        forward_kernel,
        out_shape=jax.ShapeDtypeStruct((near, flat_rows, 128), BF16),
        in_specs=[hbm] * 5,
        out_specs=pl.BlockSpec(memory_space=pltpu.VMEM),
        scratch_shapes=[
            pltpu.SMEM(src_block.shape[1:], jnp.int32),
            pltpu.SMEM(src_block.shape[1:], jnp.int32),
            pltpu.VMEM((surf, columns), BF16),
            pltpu.VMEM((levels, columns), BF16),
            pltpu.VMEM((near, width, across), BF16),
            pltpu.VMEM((32, columns), F32),
            pltpu.VMEM((columns // width, 32, width), BF16),
            pltpu.VMEM((tiles + 1, ROWS, 128), F32),
            dma((4,)),
            dma((near,)),
        ],
        compiler_params=pltpu.CompilerParams(vmem_limit_bytes=32 * 2**20),
        name="pieces",
    )(*[pltpu.with_memory_space_constraint(x, pltpu.HBM) for x in (src_block, dst_block, atm_surface, atm_levels, margin_weights)])

    vmem = pl.BlockSpec(memory_space=pltpu.VMEM)
    ocean_surface, ocean_levels, fluxes = pl.pallas_call(
        functools.partial(middle_kernel, grp_n, dom_n, lev_n),
        out_shape=[
            jax.ShapeDtypeStruct((surf, cells), F32),
            jax.ShapeDtypeStruct((levels, cells), F32),
            jax.ShapeDtypeStruct((near, tiles * surf, 128), BF16),
        ],
        in_specs=[vmem] * 5 + [pl.BlockSpec(memory_space=pltpu.SMEM), vmem],
        out_specs=[vmem] * 3,
        scratch_shapes=[
            pltpu.VMEM((4, flat_rows, 128), BF16),
            pltpu.VMEM((3, flat_rows, 128), BF16),
            pltpu.VMEM((3, flat_rows, 128), BF16),
            pltpu.VMEM((32, cells), BF16),
            pltpu.VMEM((32, 2 * HW), BF16),
            pltpu.VMEM((neighbours.shape[1], cells), jnp.int32),
            pltpu.VMEM((neighbours.shape[1], cells), jnp.int32),
            pltpu.VMEM((cells + 2 * HW, cells), BF16),
            pltpu.VMEM((32, cells), F32),
            pltpu.VMEM((8, cells), F32),
            pltpu.VMEM((8, cells), F32),
            pltpu.VMEM((ROWS, 128), F32),
            pltpu.VMEM((tiles * surf, 128), F32),
            pltpu.VMEM((tiles * surf, 128), BF16),
            pltpu.VMEM((near - 1, tiles * surf, 128), BF16),
            pltpu.VMEM((1, cells), F32),
            pltpu.VMEM((max(lev_n - 1, 1), 1, cells), F32),
            dma((4,)), dma((4,)),
            dma((3,)), dma((3,)),
            dma((2,)), dma((2,)),
            dma((3,)), dma((3,)),
            dma((near - 1,)), dma((near - 1,)),
        ],
        compiler_params=pltpu.CompilerParams(collective_id=0, has_side_effects=True, vmem_limit_bytes=48 * 2**20),
        name="middle",
    )(agg, ice_cover.reshape(1, cells), ice_flux, ocean_state, drag.reshape(1, cells), level_weights, neighbours.T)

    atm_flux, ocean_surface, ocean_levels = pl.pallas_call(
        back_kernel,
        out_shape=[
            jax.ShapeDtypeStruct((surf, columns), F32),
            jax.ShapeDtypeStruct((surf, cells), F32),
            jax.ShapeDtypeStruct((levels, cells), F32),
        ],
        in_specs=[hbm] * 2 + [vmem] * 4,
        out_specs=[vmem, hbm, hbm],
        scratch_shapes=[
            pltpu.SMEM(src_block.shape[1:], jnp.int32),
            pltpu.SMEM(src_block.shape[1:], jnp.int32),
            pltpu.VMEM((near, tiles * surf, 128), F32),
            pltpu.VMEM((near * (cells // width + 1), 8, 128), F32),
            pltpu.VMEM((near * (cells // width + 1), 8, 128), F32),
            pltpu.VMEM((4, columns // width, 8, width), F32),
            dma((4,)),
        ],
        compiler_params=pltpu.CompilerParams(vmem_limit_bytes=32 * 2**20),
        name="back",
    )(src_block, dst_block, fluxes, margin_weights, ocean_surface, ocean_levels)
    return ocean_surface, ocean_levels, atm_flux


def solution(mesh):
    return jax.shard_map(
        functools.partial(shards, mesh.shape["grp"], mesh.shape["dom"], mesh.shape["lev"]),
        mesh=mesh,
        in_specs=(
            P("lev", ("grp", "dom")),
            P("lev", ("grp", "dom")),
            P(("grp", "dom"), None, None, None),
            P(("grp", "dom"), None, None),
            P(("grp", "dom"), None, None),
            P(("grp", "dom")),
            P("lev", ("grp", "dom")),
            P("lev", ("grp", "dom")),
            P(("grp", "dom")),
            P("lev"),
            P(("grp", "dom"), None),
        ),
        out_specs=(P("lev", ("grp", "dom")), P("lev", ("grp", "dom")), P("lev", ("grp", "dom"))),
        check_vma=False,
    )
```

```python
import functools

import jax
import jax.numpy as jnp
from jax import lax
from jax.experimental import pallas as pl
from jax.experimental.pallas import tpu as pltpu
from jax.sharding import PartitionSpec as P

HW = 128
KAPPA = 0.5
ROWS = 24
MESH = pl.DeviceIdType.MESH
F32 = jnp.float32
BF16 = jnp.bfloat16


def dot(a, b):
    return jnp.dot(a, b, preferred_element_type=F32)


def forward_kernel(src_hbm, dst_hbm, surf_hbm, lev_hbm, w_hbm, out_ref, src, dst, surf_ref, lev_ref, w_ref, joint, blocks, sums, small, big):
    levels, surf = lev_ref.shape[0], surf_ref.shape[0]
    near, width, across = w_ref.shape
    slots = across // width
    tiles = sums.shape[0] - 1
    arriving = [
        pltpu.make_async_copy(here, there, small.at[n])
        for n, (here, there) in enumerate([(lev_hbm, lev_ref), (surf_hbm, surf_ref), (src_hbm.at[0], src), (dst_hbm.at[0], dst)])
    ]
    weights = [pltpu.make_async_copy(w_hbm.at[0, o], w_ref.at[o], big.at[o]) for o in range(near)]
    for one in arriving + weights:
        one.start()
    joint[levels + surf :, :] = jnp.zeros_like(joint[levels + surf :, :])
    arriving[0].wait()
    arriving[1].wait()
    joint[0:levels, :] = lev_ref[...].astype(F32)
    joint[levels : levels + surf, :] = surf_ref[...].astype(F32)
    for pair in range(blocks.shape[0] // 2):
        both = joint[:, pair * 128 : pair * 128 + 128].astype(BF16)
        blocks[2 * pair] = both[:, :64]
        blocks[2 * pair + 1] = both[:, 64:]
    arriving[2].wait()
    arriving[3].wait()
    side = lax.broadcasted_iota(jnp.int32, (ROWS, 128), 1) >> 6

    def offset(o, carry):
        pltpu.make_async_copy(w_hbm.at[0, o], w_ref.at[o], big.at[o]).wait()
        sums[...] = jnp.zeros_like(sums)
        for pair in range(slots // 2):
            slot = 2 * pair
            lhs = jnp.concatenate([blocks[src[o, slot]], blocks[src[o, slot + 1]]], axis=0)
            got = dot(lhs, w_ref[o, :, pair * 128 : pair * 128 + 128])
            for u in range(2):
                to = dst[o, slot + u]
                tile = jnp.where(to < 0, tiles, to >> 1)
                to_side = to & 1
                one = got[32 * u : 32 * u + ROWS].astype(BF16).astype(F32)
                one = pltpu.roll(one, 64 * (to_side ^ u), 1)
                sums[tile] = sums[tile] + jnp.where(side == to_side, one, 0.0)
        for t in range(0, tiles, 2):
            both = jnp.concatenate([sums[t], sums[t + 1]], axis=0)
            out_ref[o, t * ROWS : (t + 2) * ROWS, :] = both.astype(BF16)
        return carry

    lax.fori_loop(0, near, offset, 0)


def middle_kernel(
    grp_n, dom_n, lev_n,
    agg, ice_cover, ice_flux, ocean_state, drag, level_weights, neighbours,
    surf_out, lev_out, flux_out,
    sib, comb, recv, own, halo, tile_of, place_of, counts, around, ice8, state8, lw_rows, flat, flux_send, flux_recv, col_send, col_recv,
    sib_s, sib_r, far_s, far_r, halo_s, halo_r, col_s, col_r, flux_s, flux_r,
):
    grp, dom, lev = lax.axis_index("grp"), lax.axis_index("dom"), lax.axis_index("lev")
    parts = grp_n * dom_n
    p = grp * dom_n + dom
    core = lax.rem(dom, 2)
    levels, surf = lev_out.shape[0], surf_out.shape[0]
    cells = lev_out.shape[1]
    tiles = cells // 128
    near = agg.shape[0]

    def part(by):
        q = lax.rem(p + by + parts, parts)
        return (q // dom_n, lax.rem(q, dom_n), lev)

    def ring(by):
        return (grp, lax.rem(dom + by + dom_n, dom_n), lev)

    def column_peer(by):
        return (grp, dom, lax.rem(lev + by, lev_n))

    sibling = (grp, dom + 1 - 2 * core, lev)

    barrier = pltpu.get_barrier_semaphore()
    greeted = 0
    for by in range(1, near):
        for sign in (1, -1):
            pl.semaphore_signal(barrier, inc=1, device_id=part(sign * by), device_id_type=MESH)
            greeted += 1
    for by in (1, -1):
        pl.semaphore_signal(barrier, inc=1, device_id=ring(by), device_id_type=MESH)
        greeted += 1
    for by in range(1, lev_n):
        pl.semaphore_signal(barrier, inc=1, device_id=column_peer(by), device_id_type=MESH)
        greeted += 1
    pl.semaphore_wait(barrier, greeted)

    def copy(src, dst, send, got, device):
        return pltpu.make_async_remote_copy(
            src_ref=src, dst_ref=dst, send_sem=send, recv_sem=got, device_id=device, device_id_type=MESH
        )

    half = agg.shape[1] // 2
    halves = [slice(0, half), slice(half, 2 * half)]
    to_core = [
        [copy(agg.at[2 * m + 1, h], sib.at[m, h], sib_s.at[m, n], sib_r.at[m, n], part(1) if m == 3 else sibling) for m in range(4)]
        for n, h in enumerate(halves)
    ]
    far1 = copy(comb.at[0], recv.at[0], far_s.at[0, 0], far_r.at[0, 0], part(2))
    far2 = [copy(comb.at[1, h], recv.at[1, h], far_s.at[1, n], far_r.at[1, n], part(4)) for n, h in enumerate(halves)]
    far3 = [copy(comb.at[2, h], recv.at[2, h], far_s.at[2, n], far_r.at[2, n], part(2)) for n, h in enumerate(halves)]
    for ms in ((3, 2), (1, 0)):
        for n in range(2):
            for m in ms:
                to_core[n][m].start()

    def wide(ref, i, n):
        return ref[i, halves[n], :].astype(F32)

    first = levels - 16
    ice8[...] = jnp.zeros_like(ice8)
    state8[...] = jnp.zeros_like(state8)
    ice8[first : first + surf, :] = ice_flux[...].astype(F32)
    state8[first : first + surf, :] = ocean_state[...].astype(F32)
    lw_rows[...] = jnp.zeros_like(lw_rows)
    for k in range(levels):
        lw_rows[k : k + 1, :] = jnp.full((1, 128), level_weights[k], F32)
    nb = neighbours.shape[0]
    place = neighbours[...] - HW
    place = jnp.where(place < 0, place + cells + 2 * HW, place)
    tile_of[...] = place >> 7
    place_of[...] = place & 127
    def count_cells(n, carry):
        lanes = pl.ds(pl.multiple_of(n * 128, 128), 128)
        row = lax.broadcasted_iota(jnp.int32, (128, 128), 0)
        spots, tile_rows = [], []
        for e in range(nb):
            spot = jnp.where(jnp.broadcast_to(place_of[e : e + 1, lanes], (128, 128)) == row, 1.0, 0.0)
            spots.append(spot.astype(BF16))
            tile_rows.append(jnp.broadcast_to(tile_of[e : e + 1, lanes], (16, 128)).astype(F32).astype(BF16))
        for h in range(counts.shape[0] // 128):
            total = None
            for e in range(nb):
                hit = tile_rows[e] == jnp.full((16, 128), h, BF16)
                term = jnp.where(jnp.concatenate([hit] * 8, axis=0), spots[e], jnp.zeros_like(spots[e]))
                total = term if total is None else total + term
            counts[h * 128 : h * 128 + 128, lanes] = total
        return carry

    lax.fori_loop(0, 5 * tiles // 16, count_cells, 0)
    for n in range(2):
        to_core[n][3].wait_recv()
        to_core[n][2].wait_recv()
        far = wide(agg, 6, n) + wide(sib, 3, n) + jnp.where(core == 0, wide(sib, 2, n), 0.0)
        comb[2, halves[n], :] = far.astype(BF16)
        far3[n].start()
    for n in range(2):
        to_core[n][1].wait_recv()
        to_core[n][0].wait_recv()
        comb[0, halves[n], :] = (wide(agg, 2, n) + wide(sib, core, n)).astype(BF16)
    far1.start()
    lax.fori_loop(5 * tiles // 16, 5 * tiles // 8, count_cells, 0)
    for n in range(2):
        far3[n].wait_recv()
        comb[1, halves[n], :] = (wide(agg, 4, n) + wide(sib, 1 + core, n) + wide(recv, 2, n)).astype(BF16)
        far2[n].start()
    lax.fori_loop(5 * tiles // 8, tiles, count_cells, 0)
    far1.wait_recv()
    far2[0].wait_recv()
    far2[1].wait_recv()

    is_surf = lax.broadcasted_iota(jnp.int32, (8, 128), 0) >= first
    def merge(t):
        rows = slice(t * ROWS, (t + 2) * ROWS)
        total = agg[0, rows, :].astype(F32) + recv[0, rows, :].astype(F32) + recv[1, rows, :].astype(F32)
        total = total + jnp.where(core == 1, sib[0, rows, :].astype(F32), 0.0)
        for u in range(2):
            lanes = slice((t + u) * 128, (t + u + 1) * 128)
            one = total[u * ROWS : (u + 1) * ROWS]
            share = ice_cover[:, lanes]
            tail = jnp.where(is_surf, (1.0 - share) * one[16:] + share * ice8[:, lanes], one[16:])
            own[:, lanes] = jnp.concatenate([one[:16], tail, jnp.zeros((8, 128), F32)], axis=0).astype(BF16)

    merge(0)
    merge(tiles - 2)
    to_prev = copy(own.at[:, 0:HW], halo.at[:, 0:HW], halo_s.at[0], halo_r.at[0], ring(-1))
    to_next = copy(own.at[:, cells - HW : cells], halo.at[:, HW : 2 * HW], halo_s.at[1], halo_r.at[1], ring(1))
    to_prev.start()
    to_next.start()
    for t in range(2, tiles - 2, 2):
        merge(t)
    for c in range(cells // 256):
        lanes = slice(c * 256, c * 256 + 256)
        around[:, lanes] = dot(own[...], counts[0:cells, lanes])
    to_prev.wait_recv()
    to_next.wait_recv()
    weight = jnp.concatenate([lw_rows[...], lw_rows[...]], axis=1)
    for c in range(cells // 256):
        lanes = slice(c * 256, c * 256 + 256)
        total = around[:, lanes] + dot(halo[...], counts[cells : cells + 2 * HW, lanes])
        forcing = (1.0 - KAPPA) * own[:, lanes].astype(F32) + (KAPPA / nb) * total
        around[:, lanes] = forcing
        col_send[:, lanes] = jnp.sum(weight * forcing[:ROWS], axis=0, keepdims=True)

    col_copies = [copy(col_send, col_recv.at[by - 1], col_s.at[by - 1], col_r.at[by - 1], column_peer(by)) for by in range(1, lev_n)]
    for one in col_copies:
        one.start()
    lev_out[...] = around[:levels, :]
    surf_out[...] = around[levels : levels + surf, :]
    for one in col_copies:
        one.wait_recv()
    column = col_send[...]
    for by in range(1, lev_n):
        column = column + col_recv[by - 1]
    flux = drag[...] * (state8[...] - around[16:ROWS, :] + column)
    for t in range(tiles):
        flat[t * surf : (t + 1) * surf, :] = flux[first : first + surf, t * 128 : t * 128 + 128]
    flux_send[...] = flat[...].astype(BF16)
    flux_copies = [copy(flux_send, flux_recv.at[o - 1], flux_s.at[o - 1], flux_r.at[o - 1], part(-o)) for o in range(1, near)]
    for one in reversed(flux_copies):
        one.start()
    flux_out[0] = flux_send[...]
    for o in range(1, near):
        flux_copies[o - 1].wait_recv()
        flux_out[o] = flux_recv[o - 1]

    for one in to_core[0] + to_core[1] + far2 + far3 + [far1, to_prev, to_next] + col_copies + flux_copies:
        one.wait_send()


def back_kernel(src_hbm, dst_hbm, flux_ref, w_ref, surf_ref, lev_ref, out_ref, surf_out, lev_out, src, dst, flat, even, odd, total, sems):
    surf = out_ref.shape[0]
    near, width, across = w_ref.shape[1:]
    slots = across // width
    count = even.shape[0] // near - 1
    copies = [
        pltpu.make_async_copy(here, there, sems.at[n])
        for n, (here, there) in enumerate([(src_hbm.at[0], src), (dst_hbm.at[0], dst), (surf_ref, surf_out), (lev_ref, lev_out)])
    ]
    for one in copies:
        one.start()
    total[...] = jnp.zeros_like(total)
    low = lax.broadcasted_iota(jnp.int32, (surf, 128), 1) < 64
    zero = jnp.zeros((surf, 128), F32)
    flat[...] = flux_ref[...].astype(F32)

    def spread(o, carry):
        base = o * (count + 1)
        even[base + count] = jnp.zeros((8, 128), F32)
        odd[base + count] = jnp.zeros((8, 128), F32)
        for t in range(count // 2):
            here = flat[o, t * surf : (t + 1) * surf, :]
            there = pltpu.roll(here, 64, 1)
            even[base + 2 * t, 0:surf, :] = jnp.where(low, here, zero)
            odd[base + 2 * t, 0:surf, :] = jnp.where(low, zero, there)
            even[base + 2 * t + 1, 0:surf, :] = jnp.where(low, there, zero)
            odd[base + 2 * t + 1, 0:surf, :] = jnp.where(low, zero, here)
        return carry

    lax.fori_loop(0, near, spread, 0)
    copies[0].wait()
    copies[1].wait()

    def offset(o, carry):
        base = o * (count + 1)
        zero = jnp.zeros((16, 128), BF16)
        for quad in range(slots // 4):
            rows = []
            for half in range(2):
                to_a, to_b = dst[o, 4 * quad + 2 * half], dst[o, 4 * quad + 2 * half + 1]
                to_a = jnp.where(to_a < 0, count, to_a)
                to_b = jnp.where(to_b < 0, count, to_b)
                rows.append(jnp.concatenate([even[base + to_a], odd[base + to_b]], axis=0).astype(BF16))
            lhs = jnp.concatenate(
                [jnp.concatenate([rows[0], zero], axis=1), jnp.concatenate([zero, rows[1]], axis=1)], axis=0
            )
            got = lax.dot_general(
                lhs, w_ref[0, o, :, quad * 256 : quad * 256 + 256], (((1,), (1,)), ((), ())), preferred_element_type=F32
            )
            for u in range(4):
                to = src[o, 4 * quad + u]
                total[u, to] = total[u, to] + got[8 * u : 8 * u + 8]
        return carry

    lax.fori_loop(0, near, offset, 0)
    def summed(b):
        return (total[0, b] + total[1, b]) + (total[2, b] + total[3, b])

    for pair in range(total.shape[1] // 2):
        both = jnp.concatenate([summed(2 * pair), summed(2 * pair + 1)], axis=1)
        out_ref[:, pair * 128 : pair * 128 + 128] = both[:surf]
    copies[2].wait()
    copies[3].wait()


def shards(
    grp_n, dom_n, lev_n,
    atm_surface, atm_levels, margin_weights, src_block, dst_block, ice_cover, ice_flux, ocean_state, drag, level_weights,
    neighbours,
):
    surf, columns = atm_surface.shape
    levels = atm_levels.shape[0]
    near, width, across = margin_weights.shape[1:]
    cells = ice_cover.shape[0]
    tiles = cells // 128
    flat_rows = tiles * ROWS
    hbm = pl.BlockSpec(memory_space=pltpu.HBM)
    dma = pltpu.SemaphoreType.DMA
    agg = pl.pallas_call(
        forward_kernel,
        out_shape=jax.ShapeDtypeStruct((near, flat_rows, 128), BF16),
        in_specs=[hbm] * 5,
        out_specs=pl.BlockSpec(memory_space=pltpu.VMEM),
        scratch_shapes=[
            pltpu.SMEM(src_block.shape[1:], jnp.int32),
            pltpu.SMEM(src_block.shape[1:], jnp.int32),
            pltpu.VMEM((surf, columns), BF16),
            pltpu.VMEM((levels, columns), BF16),
            pltpu.VMEM((near, width, across), BF16),
            pltpu.VMEM((32, columns), F32),
            pltpu.VMEM((columns // width, 32, width), BF16),
            pltpu.VMEM((tiles + 1, ROWS, 128), F32),
            dma((4,)),
            dma((near,)),
        ],
        compiler_params=pltpu.CompilerParams(vmem_limit_bytes=32 * 2**20),
        name="pieces",
    )(*[pltpu.with_memory_space_constraint(x, pltpu.HBM) for x in (src_block, dst_block, atm_surface, atm_levels, margin_weights)])

    vmem = pl.BlockSpec(memory_space=pltpu.VMEM)
    ocean_surface, ocean_levels, fluxes = pl.pallas_call(
        functools.partial(middle_kernel, grp_n, dom_n, lev_n),
        out_shape=[
            jax.ShapeDtypeStruct((surf, cells), F32),
            jax.ShapeDtypeStruct((levels, cells), F32),
            jax.ShapeDtypeStruct((near, tiles * surf, 128), BF16),
        ],
        in_specs=[vmem] * 5 + [pl.BlockSpec(memory_space=pltpu.SMEM), vmem],
        out_specs=[vmem] * 3,
        scratch_shapes=[
            pltpu.VMEM((4, flat_rows, 128), BF16),
            pltpu.VMEM((3, flat_rows, 128), BF16),
            pltpu.VMEM((3, flat_rows, 128), BF16),
            pltpu.VMEM((32, cells), BF16),
            pltpu.VMEM((32, 2 * HW), BF16),
            pltpu.VMEM((neighbours.shape[1], cells), jnp.int32),
            pltpu.VMEM((neighbours.shape[1], cells), jnp.int32),
            pltpu.VMEM((cells + 2 * HW, cells), BF16),
            pltpu.VMEM((32, cells), F32),
            pltpu.VMEM((8, cells), F32),
            pltpu.VMEM((8, cells), F32),
            pltpu.VMEM((ROWS, 128), F32),
            pltpu.VMEM((tiles * surf, 128), F32),
            pltpu.VMEM((tiles * surf, 128), BF16),
            pltpu.VMEM((near - 1, tiles * surf, 128), BF16),
            pltpu.VMEM((1, cells), F32),
            pltpu.VMEM((max(lev_n - 1, 1), 1, cells), F32),
            dma((4, 2)), dma((4, 2)),
            dma((3, 2)), dma((3, 2)),
            dma((2,)), dma((2,)),
            dma((3,)), dma((3,)),
            dma((near - 1,)), dma((near - 1,)),
        ],
        compiler_params=pltpu.CompilerParams(collective_id=0, has_side_effects=True, vmem_limit_bytes=48 * 2**20),
        name="middle",
    )(agg, ice_cover.reshape(1, cells), ice_flux, ocean_state, drag.reshape(1, cells), level_weights, neighbours.T)

    atm_flux, ocean_surface, ocean_levels = pl.pallas_call(
        back_kernel,
        out_shape=[
            jax.ShapeDtypeStruct((surf, columns), F32),
            jax.ShapeDtypeStruct((surf, cells), F32),
            jax.ShapeDtypeStruct((levels, cells), F32),
        ],
        in_specs=[hbm] * 2 + [vmem] * 4,
        out_specs=[vmem, hbm, hbm],
        scratch_shapes=[
            pltpu.SMEM(src_block.shape[1:], jnp.int32),
            pltpu.SMEM(src_block.shape[1:], jnp.int32),
            pltpu.VMEM((near, tiles * surf, 128), F32),
            pltpu.VMEM((near * (cells // width + 1), 8, 128), F32),
            pltpu.VMEM((near * (cells // width + 1), 8, 128), F32),
            pltpu.VMEM((4, columns // width, 8, width), F32),
            dma((4,)),
        ],
        compiler_params=pltpu.CompilerParams(vmem_limit_bytes=32 * 2**20),
        name="back",
    )(src_block, dst_block, fluxes, margin_weights, ocean_surface, ocean_levels)
    return ocean_surface, ocean_levels, atm_flux


def solution(mesh):
    return jax.shard_map(
        functools.partial(shards, mesh.shape["grp"], mesh.shape["dom"], mesh.shape["lev"]),
        mesh=mesh,
        in_specs=(
            P("lev", ("grp", "dom")),
            P("lev", ("grp", "dom")),
            P(("grp", "dom"), None, None, None),
            P(("grp", "dom"), None, None),
            P(("grp", "dom"), None, None),
            P(("grp", "dom")),
            P("lev", ("grp", "dom")),
            P("lev", ("grp", "dom")),
            P(("grp", "dom")),
            P("lev"),
            P(("grp", "dom"), None),
        ),
        out_specs=(P("lev", ("grp", "dom")), P("lev", ("grp", "dom")), P("lev", ("grp", "dom"))),
        check_vma=False,
    )
```

```python
import functools

import jax
import jax.numpy as jnp
from jax import lax
from jax.experimental import pallas as pl
from jax.experimental.pallas import tpu as pltpu
from jax.sharding import PartitionSpec as P

HW = 128
KAPPA = 0.5
ROWS = 24
MESH = pl.DeviceIdType.MESH
F32 = jnp.float32
BF16 = jnp.bfloat16


def dot(a, b):
    return jnp.dot(a, b, preferred_element_type=F32)


def forward_kernel(src_hbm, dst_hbm, surf_hbm, lev_hbm, w_hbm, out_ref, src, dst, surf_ref, lev_ref, w_ref, joint, blocks, sums, small, big):
    levels, surf = lev_ref.shape[0], surf_ref.shape[0]
    near, width, across = w_ref.shape
    slots = across // width
    tiles = sums.shape[0] - 1
    arriving = [
        pltpu.make_async_copy(here, there, small.at[n])
        for n, (here, there) in enumerate([(lev_hbm, lev_ref), (surf_hbm, surf_ref), (src_hbm.at[0], src), (dst_hbm.at[0], dst)])
    ]
    weights = [pltpu.make_async_copy(w_hbm.at[0, o], w_ref.at[o], big.at[o]) for o in range(near)]
    for one in arriving + weights:
        one.start()
    joint[levels + surf :, :] = jnp.zeros_like(joint[levels + surf :, :])
    arriving[0].wait()
    arriving[1].wait()
    joint[0:levels, :] = lev_ref[...].astype(F32)
    joint[levels : levels + surf, :] = surf_ref[...].astype(F32)
    for pair in range(blocks.shape[0] // 2):
        both = joint[:, pair * 128 : pair * 128 + 128].astype(BF16)
        blocks[2 * pair] = both[:, :64]
        blocks[2 * pair + 1] = both[:, 64:]
    arriving[2].wait()
    arriving[3].wait()
    side = lax.broadcasted_iota(jnp.int32, (ROWS, 128), 1) >> 6

    def offset(o, carry):
        pltpu.make_async_copy(w_hbm.at[0, o], w_ref.at[o], big.at[o]).wait()
        sums[...] = jnp.zeros_like(sums)
        for pair in range(slots // 2):
            slot = 2 * pair
            lhs = jnp.concatenate([blocks[src[o, slot]], blocks[src[o, slot + 1]]], axis=0)
            got = dot(lhs, w_ref[o, :, pair * 128 : pair * 128 + 128])
            for u in range(2):
                to = dst[o, slot + u]
                tile = jnp.where(to < 0, tiles, to >> 1)
                to_side = to & 1
                one = got[32 * u : 32 * u + ROWS].astype(BF16).astype(F32)
                one = pltpu.roll(one, 64 * (to_side ^ u), 1)
                sums[tile] = sums[tile] + jnp.where(side == to_side, one, 0.0)
        for t in range(0, tiles, 2):
            both = jnp.concatenate([sums[t], sums[t + 1]], axis=0)
            out_ref[o, t * ROWS : (t + 2) * ROWS, :] = both.astype(BF16)
        return carry

    lax.fori_loop(0, near, offset, 0)


def middle_kernel(
    grp_n, dom_n, lev_n,
    agg, ice_cover, ice_flux, ocean_state, drag, level_weights, neighbours,
    surf_out, lev_out, flux_out,
    sib, comb, recv, own, halo, tile_of, place_of, counts, around, ice8, state8, lw_rows, flat, flux_send, flux_recv, col_send, col_recv,
    sib_s, sib_r, far_s, far_r, halo_s, halo_r, col_s, col_r, flux_s, flux_r,
):
    grp, dom, lev = lax.axis_index("grp"), lax.axis_index("dom"), lax.axis_index("lev")
    parts = grp_n * dom_n
    p = grp * dom_n + dom
    core = lax.rem(dom, 2)
    levels, surf = lev_out.shape[0], surf_out.shape[0]
    cells = lev_out.shape[1]
    tiles = cells // 128
    near = agg.shape[0]

    def part(by):
        q = lax.rem(p + by + parts, parts)
        return (q // dom_n, lax.rem(q, dom_n), lev)

    def ring(by):
        return (grp, lax.rem(dom + by + dom_n, dom_n), lev)

    def column_peer(by):
        return (grp, dom, lax.rem(lev + by, lev_n))

    sibling = (grp, dom + 1 - 2 * core, lev)

    barrier = pltpu.get_barrier_semaphore()
    greeted = 0
    for by in range(1, near):
        for sign in (1, -1):
            pl.semaphore_signal(barrier, inc=1, device_id=part(sign * by), device_id_type=MESH)
            greeted += 1
    for by in (1, -1):
        pl.semaphore_signal(barrier, inc=1, device_id=ring(by), device_id_type=MESH)
        greeted += 1
    for by in range(1, lev_n):
        pl.semaphore_signal(barrier, inc=1, device_id=column_peer(by), device_id_type=MESH)
        greeted += 1
    pl.semaphore_wait(barrier, greeted)

    def copy(src, dst, send, got, device):
        return pltpu.make_async_remote_copy(
            src_ref=src, dst_ref=dst, send_sem=send, recv_sem=got, device_id=device, device_id_type=MESH
        )

    sib_copies = [copy(agg.at[2 * m + 1], sib.at[m], sib_s.at[m], sib_r.at[m], sibling) for m in range(3)]
    sib_copies.append(copy(agg.at[7], sib.at[3], sib_s.at[3], sib_r.at[3], part(1)))
    far1 = copy(comb.at[0], recv.at[0], far_s.at[0], far_r.at[0], part(2))
    far2 = copy(comb.at[1], recv.at[1], far_s.at[1], far_r.at[1], part(4))
    far3 = copy(comb.at[2], recv.at[2], far_s.at[2], far_r.at[2], part(2))
    for m in reversed(range(4)):
        sib_copies[m].start()

    def wide(ref, n):
        return ref[n].astype(F32)

    first = levels - 16
    ice8[...] = jnp.zeros_like(ice8)
    state8[...] = jnp.zeros_like(state8)
    ice8[first : first + surf, :] = ice_flux[...].astype(F32)
    state8[first : first + surf, :] = ocean_state[...].astype(F32)
    lw_rows[...] = jnp.zeros_like(lw_rows)
    for k in range(levels):
        lw_rows[k : k + 1, :] = jnp.full((1, 128), level_weights[k], F32)
    nb = neighbours.shape[0]
    place = neighbours[...] - HW
    place = jnp.where(place < 0, place + cells + 2 * HW, place)
    tile_of[...] = place >> 7
    place_of[...] = place & 127
    def count_cells(n, carry):
        lanes = pl.ds(pl.multiple_of(n * 128, 128), 128)
        row = lax.broadcasted_iota(jnp.int32, (128, 128), 0)
        spots, tile_rows = [], []
        for e in range(nb):
            spot = jnp.where(jnp.broadcast_to(place_of[e : e + 1, lanes], (128, 128)) == row, 1.0, 0.0)
            spots.append(spot.astype(BF16))
            tile_rows.append(jnp.broadcast_to(tile_of[e : e + 1, lanes], (16, 128)).astype(F32).astype(BF16))
        for h in range(counts.shape[0] // 128):
            total = None
            for e in range(nb):
                hit = tile_rows[e] == jnp.full((16, 128), h, BF16)
                term = jnp.where(jnp.concatenate([hit] * 8, axis=0), spots[e], jnp.zeros_like(spots[e]))
                total = term if total is None else total + term
            counts[h * 128 : h * 128 + 128, lanes] = total
        return carry

    lax.fori_loop(0, tiles // 8, count_cells, 0)
    sib_copies[3].wait_recv()
    sib_copies[2].wait_recv()
    comb[2] = (wide(agg, 6) + wide(sib, 3) + jnp.where(core == 0, wide(sib, 2), 0.0)).astype(BF16)
    far3.start()
    sib_copies[1].wait_recv()
    sib_copies[0].wait_recv()
    comb[0] = (wide(agg, 2) + wide(sib, core)).astype(BF16)
    far1.start()

    lax.fori_loop(tiles // 8, tiles // 4, count_cells, 0)
    far3.wait_recv()
    comb[1] = (wide(agg, 4) + wide(sib, 1 + core) + wide(recv, 2)).astype(BF16)
    far2.start()
    lax.fori_loop(tiles // 4, tiles, count_cells, 0)

    far1.wait_recv()
    far2.wait_recv()

    is_surf = lax.broadcasted_iota(jnp.int32, (8, 128), 0) >= first
    def merge(t):
        rows = slice(t * ROWS, (t + 2) * ROWS)
        total = agg[0, rows, :].astype(F32) + recv[0, rows, :].astype(F32) + recv[1, rows, :].astype(F32)
        total = total + jnp.where(core == 1, sib[0, rows, :].astype(F32), 0.0)
        for u in range(2):
            lanes = slice((t + u) * 128, (t + u + 1) * 128)
            one = total[u * ROWS : (u + 1) * ROWS]
            share = ice_cover[:, lanes]
            tail = jnp.where(is_surf, (1.0 - share) * one[16:] + share * ice8[:, lanes], one[16:])
            own[:, lanes] = jnp.concatenate([one[:16], tail, jnp.zeros((8, 128), F32)], axis=0).astype(BF16)

    merge(0)
    merge(tiles - 2)
    to_prev = copy(own.at[:, 0:HW], halo.at[:, 0:HW], halo_s.at[0], halo_r.at[0], ring(-1))
    to_next = copy(own.at[:, cells - HW : cells], halo.at[:, HW : 2 * HW], halo_s.at[1], halo_r.at[1], ring(1))
    to_prev.start()
    to_next.start()
    for t in range(2, tiles - 2, 2):
        merge(t)
    for c in range(cells // 256):
        lanes = slice(c * 256, c * 256 + 256)
        around[:, lanes] = dot(own[...], counts[0:cells, lanes])
    to_prev.wait_recv()
    to_next.wait_recv()
    weight = jnp.concatenate([lw_rows[...], lw_rows[...]], axis=1)
    for c in range(cells // 256):
        lanes = slice(c * 256, c * 256 + 256)
        total = around[:, lanes] + dot(halo[...], counts[cells : cells + 2 * HW, lanes])
        forcing = (1.0 - KAPPA) * own[:, lanes].astype(F32) + (KAPPA / nb) * total
        around[:, lanes] = forcing
        col_send[:, lanes] = jnp.sum(weight * forcing[:ROWS], axis=0, keepdims=True)

    col_copies = [copy(col_send, col_recv.at[by - 1], col_s.at[by - 1], col_r.at[by - 1], column_peer(by)) for by in range(1, lev_n)]
    for one in col_copies:
        one.start()
    lev_out[...] = around[:levels, :]
    surf_out[...] = around[levels : levels + surf, :]
    for one in col_copies:
        one.wait_recv()
    column = col_send[...]
    for by in range(1, lev_n):
        column = column + col_recv[by - 1]
    flux = drag[...] * (state8[...] - around[16:ROWS, :] + column)
    for t in range(tiles):
        flat[t * surf : (t + 1) * surf, :] = flux[first : first + surf, t * 128 : t * 128 + 128]
    flux_send[...] = flat[...].astype(BF16)
    flux_copies = [copy(flux_send, flux_recv.at[o - 1], flux_s.at[o - 1], flux_r.at[o - 1], part(-o)) for o in range(1, near)]
    for one in reversed(flux_copies):
        one.start()
    flux_out[0] = flux_send[...]
    for o in range(1, near):
        flux_copies[o - 1].wait_recv()
        flux_out[o] = flux_recv[o - 1]

    for one in sib_copies + [far1, far2, far3, to_prev, to_next] + col_copies + flux_copies:
        one.wait_send()


def back_kernel(src_hbm, dst_hbm, flux_ref, w_ref, surf_ref, lev_ref, out_ref, surf_out, lev_out, src, dst, flat, even, odd, total, sems):
    surf = out_ref.shape[0]
    near, width, across = w_ref.shape[1:]
    slots = across // width
    count = even.shape[0] // near - 1
    copies = [
        pltpu.make_async_copy(here, there, sems.at[n])
        for n, (here, there) in enumerate([(src_hbm.at[0], src), (dst_hbm.at[0], dst), (surf_ref, surf_out), (lev_ref, lev_out)])
    ]
    for one in copies:
        one.start()
    total[...] = jnp.zeros_like(total)
    low = lax.broadcasted_iota(jnp.int32, (surf, 128), 1) < 64
    zero = jnp.zeros((surf, 128), F32)
    flat[...] = flux_ref[...].astype(F32)

    def spread(o, carry):
        base = o * (count + 1)
        even[base + count] = jnp.zeros((8, 128), F32)
        odd[base + count] = jnp.zeros((8, 128), F32)
        for t in range(count // 2):
            here = flat[o, t * surf : (t + 1) * surf, :]
            there = pltpu.roll(here, 64, 1)
            even[base + 2 * t, 0:surf, :] = jnp.where(low, here, zero)
            odd[base + 2 * t, 0:surf, :] = jnp.where(low, zero, there)
            even[base + 2 * t + 1, 0:surf, :] = jnp.where(low, there, zero)
            odd[base + 2 * t + 1, 0:surf, :] = jnp.where(low, zero, here)
        return carry

    lax.fori_loop(0, near, spread, 0)
    copies[0].wait()
    copies[1].wait()

    def offset(o, carry):
        base = o * (count + 1)
        zero = jnp.zeros((16, 128), BF16)
        for quad in range(slots // 4):
            rows = []
            for half in range(2):
                to_a, to_b = dst[o, 4 * quad + 2 * half], dst[o, 4 * quad + 2 * half + 1]
                to_a = jnp.where(to_a < 0, count, to_a)
                to_b = jnp.where(to_b < 0, count, to_b)
                rows.append(jnp.concatenate([even[base + to_a], odd[base + to_b]], axis=0).astype(BF16))
            lhs = jnp.concatenate(
                [jnp.concatenate([rows[0], zero], axis=1), jnp.concatenate([zero, rows[1]], axis=1)], axis=0
            )
            got = lax.dot_general(
                lhs, w_ref[0, o, :, quad * 256 : quad * 256 + 256], (((1,), (1,)), ((), ())), preferred_element_type=F32
            )
            for u in range(4):
                to = src[o, 4 * quad + u]
                total[u, to] = total[u, to] + got[8 * u : 8 * u + 8]
        return carry

    lax.fori_loop(0, near, offset, 0)
    def summed(b):
        return (total[0, b] + total[1, b]) + (total[2, b] + total[3, b])

    for pair in range(total.shape[1] // 2):
        both = jnp.concatenate([summed(2 * pair), summed(2 * pair + 1)], axis=1)
        out_ref[:, pair * 128 : pair * 128 + 128] = both[:surf]
    copies[2].wait()
    copies[3].wait()


def shards(
    grp_n, dom_n, lev_n,
    atm_surface, atm_levels, margin_weights, src_block, dst_block, ice_cover, ice_flux, ocean_state, drag, level_weights,
    neighbours,
):
    surf, columns = atm_surface.shape
    levels = atm_levels.shape[0]
    near, width, across = margin_weights.shape[1:]
    cells = ice_cover.shape[0]
    tiles = cells // 128
    flat_rows = tiles * ROWS
    hbm = pl.BlockSpec(memory_space=pltpu.HBM)
    dma = pltpu.SemaphoreType.DMA
    agg = pl.pallas_call(
        forward_kernel,
        out_shape=jax.ShapeDtypeStruct((near, flat_rows, 128), BF16),
        in_specs=[hbm] * 5,
        out_specs=pl.BlockSpec(memory_space=pltpu.VMEM),
        scratch_shapes=[
            pltpu.SMEM(src_block.shape[1:], jnp.int32),
            pltpu.SMEM(src_block.shape[1:], jnp.int32),
            pltpu.VMEM((surf, columns), BF16),
            pltpu.VMEM((levels, columns), BF16),
            pltpu.VMEM((near, width, across), BF16),
            pltpu.VMEM((32, columns), F32),
            pltpu.VMEM((columns // width, 32, width), BF16),
            pltpu.VMEM((tiles + 1, ROWS, 128), F32),
            dma((4,)),
            dma((near,)),
        ],
        compiler_params=pltpu.CompilerParams(vmem_limit_bytes=32 * 2**20),
        name="pieces",
    )(*[pltpu.with_memory_space_constraint(x, pltpu.HBM) for x in (src_block, dst_block, atm_surface, atm_levels, margin_weights)])

    vmem = pl.BlockSpec(memory_space=pltpu.VMEM)
    ocean_surface, ocean_levels, fluxes = pl.pallas_call(
        functools.partial(middle_kernel, grp_n, dom_n, lev_n),
        out_shape=[
            jax.ShapeDtypeStruct((surf, cells), F32),
            jax.ShapeDtypeStruct((levels, cells), F32),
            jax.ShapeDtypeStruct((near, tiles * surf, 128), BF16),
        ],
        in_specs=[vmem] * 5 + [pl.BlockSpec(memory_space=pltpu.SMEM), vmem],
        out_specs=[vmem] * 3,
        scratch_shapes=[
            pltpu.VMEM((4, flat_rows, 128), BF16),
            pltpu.VMEM((3, flat_rows, 128), BF16),
            pltpu.VMEM((3, flat_rows, 128), BF16),
            pltpu.VMEM((32, cells), BF16),
            pltpu.VMEM((32, 2 * HW), BF16),
            pltpu.VMEM((neighbours.shape[1], cells), jnp.int32),
            pltpu.VMEM((neighbours.shape[1], cells), jnp.int32),
            pltpu.VMEM((cells + 2 * HW, cells), BF16),
            pltpu.VMEM((32, cells), F32),
            pltpu.VMEM((8, cells), F32),
            pltpu.VMEM((8, cells), F32),
            pltpu.VMEM((ROWS, 128), F32),
            pltpu.VMEM((tiles * surf, 128), F32),
            pltpu.VMEM((tiles * surf, 128), BF16),
            pltpu.VMEM((near - 1, tiles * surf, 128), BF16),
            pltpu.VMEM((1, cells), F32),
            pltpu.VMEM((max(lev_n - 1, 1), 1, cells), F32),
            dma((4,)), dma((4,)),
            dma((3,)), dma((3,)),
            dma((2,)), dma((2,)),
            dma((3,)), dma((3,)),
            dma((near - 1,)), dma((near - 1,)),
        ],
        compiler_params=pltpu.CompilerParams(collective_id=0, has_side_effects=True, vmem_limit_bytes=48 * 2**20),
        name="middle",
    )(agg, ice_cover.reshape(1, cells), ice_flux, ocean_state, drag.reshape(1, cells), level_weights, neighbours.T)

    atm_flux, ocean_surface, ocean_levels = pl.pallas_call(
        back_kernel,
        out_shape=[
            jax.ShapeDtypeStruct((surf, columns), F32),
            jax.ShapeDtypeStruct((surf, cells), F32),
            jax.ShapeDtypeStruct((levels, cells), F32),
        ],
        in_specs=[hbm] * 2 + [vmem] * 4,
        out_specs=[vmem, hbm, hbm],
        scratch_shapes=[
            pltpu.SMEM(src_block.shape[1:], jnp.int32),
            pltpu.SMEM(src_block.shape[1:], jnp.int32),
            pltpu.VMEM((near, tiles * surf, 128), F32),
            pltpu.VMEM((near * (cells // width + 1), 8, 128), F32),
            pltpu.VMEM((near * (cells // width + 1), 8, 128), F32),
            pltpu.VMEM((4, columns // width, 8, width), F32),
            dma((4,)),
        ],
        compiler_params=pltpu.CompilerParams(vmem_limit_bytes=32 * 2**20),
        name="back",
    )(src_block, dst_block, fluxes, margin_weights, ocean_surface, ocean_levels)
    return ocean_surface, ocean_levels, atm_flux


def solution(mesh):
    return jax.shard_map(
        functools.partial(shards, mesh.shape["grp"], mesh.shape["dom"], mesh.shape["lev"]),
        mesh=mesh,
        in_specs=(
            P("lev", ("grp", "dom")),
            P("lev", ("grp", "dom")),
            P(("grp", "dom"), None, None, None),
            P(("grp", "dom"), None, None),
            P(("grp", "dom"), None, None),
            P(("grp", "dom")),
            P("lev", ("grp", "dom")),
            P("lev", ("grp", "dom")),
            P(("grp", "dom")),
            P("lev"),
            P(("grp", "dom"), None),
        ),
        out_specs=(P("lev", ("grp", "dom")), P("lev", ("grp", "dom")), P("lev", ("grp", "dom"))),
        check_vma=False,
    )
```
